128 devices in a mesh: tm: 8 (over x, core), space: 16 (over y, z).
Axes of the slice: x: 4, y: 4, z: 4, core: 2. Of those that a mesh axis runs over, the one named last changes fastest.
Arguments:
- frames: bfloat16 [16, 768, 48, 384], P('tm', 'space'), may hold values from -6 to 6
- peak_voxels: int32 [4, 3, 8, 240], P(None, None, 'tm', 'space'), may hold values from -15 to 15
- owners: int32 [7680, 1], P(('tm', 'space')), may hold values from 0 to 127; in each aligned block of 60 rows (0 to 59, 60 to 119, ...) at most 3 rows name the same one
- tile_cells: int32 [7680], P(('tm', 'space')), may hold values from 0 to 127
Outputs:
- velocity: float32 [4, 3, 8, 240], P(None, None, 'tm', 'space')
- tile_velocity: float32 [3, 16384], P(None, ('tm', 'space'))
The draws below stay inside these ranges and needn't reach their ends.
Inputs may be any that keep to these rules, and one draw needn't show every extreme that they name: `owners`: in each aligned block of 60 rows (the rows of one device) at most 3 rows name the same owner; some owner is named by exactly 3 rows of a block.
All inputs are finite; a program needn't handle non-finite values.
Results may differ from the reference program's by a relative error of at most 0.0003.
Values may be sent and summed in bfloat16 or wider, within the bound.
A program may use at most 320 MiB of HBM per device.

```python
import math
import jax
import jax.numpy as jnp
import numpy as np
from jax import lax

W = 48
H = 16
WY = 1
WZ = 15
GAPS = 4
TCELLS = 128
S = 24
NY = 48
NZ = 384
NX = 768
FRAMES = 16
FPD = 2
PD = 1
PAIRS = 8
NWIN = 240
ROWS_DEV = 60
CAP = 3
VECS = 7680
N_TM = 8
N_SPACE = 16
DEVICES = 128


def touch_ends(result, rng, low, high):
    longest = result.shape.index(max(result.shape))
    spots = []
    for shift in (0, 1):
        where = [jax.random.randint(jax.random.fold_in(rng, axis), (), 0, length) for axis, length in enumerate(result.shape)]
        where[longest] = (where[longest] + shift) % result.shape[longest]
        spots.append(tuple(where))
    return result.at[spots[0]].set(low).at[spots[1]].set(high)


def levels(stream_key, extent, shards, smallest, largest):
    factor_of, own = 1.0, jax.random.fold_in(stream_key, 6)
    for dim, shards_of in shards:
        steps = jnp.exp(jax.random.uniform(jax.random.fold_in(own, dim), (shards_of,), jnp.float32, smallest / len(shards), largest / len(shards)))
        factor_of = factor_of * jnp.repeat(steps, extent[dim] // shards_of).reshape([-1 if axis == dim else 1 for axis in range(len(extent))])
    return factor_of


def assign_block(stream_key, own, number, rows, number_of, top, limit, skew):
    ranking = jax.random.permutation(stream_key, number_of)
    packed, common = shares(number_of, rows * top, limit, skew, True), shares(number_of, rows * top, limit, skew, False)
    places = jnp.arange(number_of)

    def named(sizes, turn):
        used = int((sizes > 0).sum())
        fixed = max(1, used // 4)
        moved = fixed + (places - fixed + turn * (used - fixed)) % max(1, number_of - fixed)
        return jnp.zeros((number_of,), jnp.int32).at[ranking[jnp.where(places < fixed, places, moved)]].set(jnp.asarray(sizes, jnp.int32))

    sizes = jnp.where(number % 4 == 0, named(packed, number // 4), named(common, number - number // 4 - 1))
    mixed = jax.random.permutation(jax.random.fold_in(own, 3), number_of)
    donor, receiver = mixed[0:number_of // 2 * 2:2], mixed[1:number_of // 2 * 2:2]
    slack = jnp.minimum(sizes[donor] - 1, limit - sizes[receiver]) // 2
    slack = jnp.where((donor == ranking[0]) | (receiver == ranking[0]) | (sizes[receiver] == 0), 0, jnp.maximum(slack, 0))
    moved = jax.random.randint(jax.random.fold_in(own, 4), (number_of // 2,), 0, 1 << 20) % (slack + 1)
    sizes = sizes.at[donor].add(-moved).at[receiver].add(moved)
    items = jnp.searchsorted(jnp.cumsum(sizes), jnp.arange(rows * top), side="right").astype(jnp.int32)
    grid = items.reshape(top, rows).T
    grid = grid[jax.random.permutation(jax.random.fold_in(own, 1), rows)]
    turn = jax.random.randint(jax.random.fold_in(own, 2), (rows, 1), 0, top)
    return jnp.take_along_axis(grid, (jnp.arange(top)[None, :] + turn) % top, axis=1)


def shares(number_of, total, most, lean, full):
    portions = [(1 << 20) // math.isqrt(standing ** lean) + 1 for standing in range(1, number_of + 1)]
    largest = most if full else min(most, max(-(-total // number_of), total * portions[0] // sum(portions)))
    least = 1 if total - largest >= number_of - 1 else 0
    given, spare = [largest] + [least] * (number_of - 1), total - largest - least * (number_of - 1)
    while spare > 0:
        free = [i for i in range(1, number_of) if given[i] < largest] or [i for i in range(1, number_of) if given[i] < most]
        pool, budget = sum([portions[i] for i in free]), spare
        for i in free:
            extra = min(most - given[i], max(1, budget * portions[i] // pool), spare)
            given[i] = given[i] + extra
            spare = spare - extra
    return np.array(given)


def gaussian(key, extent, deviation, reach, shards=(), kind=jnp.bfloat16):
    drawn = deviation * jax.random.normal(key, extent, jnp.float32)
    if shards:
        drawn = drawn * levels(key, extent, shards, -0.22, 0.18)
    return jnp.clip(drawn, -reach, reach).astype(kind)


def setup_inputs(seed: int = 0) -> dict:
    key_of = jax.random.split(jax.random.key(seed), 5)
    frames = gaussian(key_of[0], (FRAMES, NX, NY, NZ), 1.0, 6.0, ((0, 8), (1, 16)))
    peak_voxels = touch_ends(jax.random.randint(key_of[1], (GAPS, 3, PAIRS, NWIN), 1 - H, H), jax.random.fold_in(key_of[1], 1), 1 - H, H - 1).astype(jnp.int32)
    owners_keys = jax.random.split(jax.random.fold_in(key_of[2], 1), VECS // ROWS_DEV)
    owners_turns = jax.random.permutation(jax.random.fold_in(key_of[2], 3), VECS // ROWS_DEV)
    owners = jax.vmap(lambda own, number: assign_block(jax.random.fold_in(key_of[2], 2), own, number, ROWS_DEV, DEVICES, 1, CAP, 2))(owners_keys, owners_turns).reshape((VECS, 1))
    tile_cells = touch_ends(jax.random.randint(key_of[3], (VECS,), 0, TCELLS), jax.random.fold_in(key_of[3], 1), 0, TCELLS - 1).astype(jnp.int32)
    return {"frames": frames, "peak_voxels": peak_voxels, "owners": owners, "tile_cells": tile_cells}


def first_frame(gap_size, slot_index):
    device_index = slot_index // PD
    place_index = slot_index % PD
    if gap_size < FPD:
        return FPD * device_index + (place_index // gap_size) * 2 * gap_size + place_index % gap_size
    tm_step = gap_size // FPD
    if (device_index // tm_step) % 2 == 0:
        return FPD * device_index + place_index
    return FPD * (device_index - tm_step) + PD + place_index


def unit_shift(axis_index, sign_value):
    return tuple(sign_value if position == axis_index else 0 for position in range(3))


def window_fits(slab_first, slab_second, peak_block, gap_size):
    window_index = jnp.arange(WY * WZ, dtype=jnp.int32)
    y_anchor = (S * (window_index // WZ)).astype(jnp.int32)
    z_anchor = (S * (window_index % WZ)).astype(jnp.int32)
    weight_norm = float(W) ** -1.5

    def single_window(y_start, z_start, x_peak, y_peak, z_peak):
        zero_index = jnp.zeros((), jnp.int32)
        block_first = lax.dynamic_slice(slab_first, (zero_index, y_start, z_start), (W, W, W)).astype(jnp.float32)
        block_second = lax.dynamic_slice(slab_second, (H - 1 + x_peak, H - 1 + y_start + y_peak, H - 1 + z_start + z_peak), (W + 2, W + 2, W + 2)).astype(jnp.float32)

        def shifted(offsets):
            piece = block_second[1 + offsets[0]:1 + offsets[0] + W, 1 + offsets[1]:1 + offsets[1] + W, 1 + offsets[2]:1 + offsets[2] + W]
            return jnp.sum(block_first * piece) * weight_norm

        centre = shifted((0, 0, 0))
        result_list = []
        for axis_index in range(3):
            lower_value = shifted(unit_shift(axis_index, -1))
            upper_value = shifted(unit_shift(axis_index, 1))
            curvature = jnp.maximum(2.0 * centre - upper_value - lower_value, 1.0)
            result_list.append(0.5 * (upper_value - lower_value) / curvature)
        return jnp.stack(result_list)

    fits = jax.vmap(single_window)(y_anchor, z_anchor, peak_block[0], peak_block[1], peak_block[2])
    return (peak_block.astype(jnp.float32) + fits.T) / gap_size


def reference(frames, peak_voxels, owners, tile_cells):
    gap_results = []
    for gap_index in range(GAPS):
        gap_size = 2 ** gap_index
        slot_results = []
        for slot_index in range(PAIRS):
            first_index = first_frame(gap_size, slot_index)
            frame_first = frames[first_index]
            frame_second = jnp.pad(frames[first_index + gap_size], ((H, H), (H, H), (H, H)))
            peak_pair = peak_voxels[gap_index, :, slot_index]

            def slab_fit(slab_index):
                slab_first = lax.dynamic_slice_in_dim(frame_first, slab_index * W, W, 0)
                slab_second = lax.dynamic_slice_in_dim(frame_second, slab_index * W, W + 2 * H, 0)
                peak_block = lax.dynamic_slice_in_dim(peak_pair, slab_index * (WY * WZ), WY * WZ, 1)
                return window_fits(slab_first, slab_second, peak_block, gap_size)

            per_slab = lax.map(slab_fit, jnp.arange(N_SPACE, dtype=jnp.int32))
            slot_results.append(jnp.transpose(per_slab, (1, 0, 2)).reshape(3, NWIN))
        gap_results.append(jnp.stack(slot_results, axis=1))
    velocity = jnp.stack(gap_results)
    listed = velocity.reshape(GAPS, 3, N_TM, PD, N_SPACE, WY * WZ)
    listed = jnp.transpose(listed, (1, 2, 4, 0, 3, 5)).reshape(3, VECS)
    segment_count = N_TM * N_SPACE * TCELLS
    target = owners[:, 0] * TCELLS + tile_cells
    cell_sums = jax.ops.segment_sum(listed.T, target, num_segments=segment_count).T
    counts = jax.ops.segment_sum(jnp.ones((VECS,), jnp.float32), target, num_segments=segment_count)
    tile_velocity = cell_sums / jnp.maximum(counts, 1.0)[None, :]
    return velocity, tile_velocity
```

```python
import functools

import jax
import jax.numpy as jnp
from jax import lax
from jax.experimental import pallas as pl
from jax.experimental.pallas import tpu as pltpu
from jax.sharding import PartitionSpec as P

W = 48
H = 16
S = 24
NWIN = 15
CELLS = 128
NS = 16
NT = 8
EXT = W + 2 * H
DEPTH = 25 * 128
BF = jnp.bfloat16
F32 = jnp.float32
MESH = pl.DeviceIdType.MESH

PASS_STEPS = {2: 3, 1: 12, 0: 20}


def lane(shape):
    return lax.broadcasted_iota(jnp.int32, shape, len(shape) - 1)


def prepare_first(planes, side, w, right):
    start = S * w
    tile = start // 128
    offset = start - 128 * tile
    here = pl.ds(pl.multiple_of(128 * tile, 128), 128)
    there = pl.ds(pl.multiple_of(128 * lax.min(tile + 1, 2), 128), 128)
    c = lane((1, 1, 128))
    d = jnp.where(c >= 64, c - 64, c + 64)
    keep = [((v >= offset) & (v < offset + W), v + 128 < offset + W) for v in (c, d)]
    zero = jnp.zeros((2, W, 128), BF)
    previous = None
    for j in range(24):
        low, high = [
            jnp.where(
                keep[r][0],
                planes[side, r, 2 * j : 2 * j + 2, :, here],
                jnp.where(keep[r][1], planes[side, r, 2 * j : 2 * j + 2, :, there], zero),
            )
            for r in range(2)
        ]
        even = low[0] + high[1]
        right[48:96, j * 128 : j * 128 + 128] = even
        right[96:144, j * 128 + 128 : j * 128 + 256] = even
        right[0:48, j * 128 : j * 128 + 128] = high[0] if previous is None else high[0] + previous
        previous = low[1]
    right[0:48, 24 * 128 :] = previous


def prepare_second(wide, side, w, qx, qz, left):
    start = S * w
    base = start - 128 * (start // 128)
    tile = (start + 112) // 128
    offset = start + qz - 1 - 128 * (tile - 1)
    here = pl.ds(pl.multiple_of(128 * lax.rem(tile + 3, 4), 128), 128)
    there = pl.ds(pl.multiple_of(128 * tile, 128), 128)
    c = lane((1, 128))
    first = c >= offset
    slot = lax.rem(c + 128 - base, 128) < 64
    turn = base - offset + 512
    for j in range(25):
        pair = [
            jnp.where(
                first,
                wide[side, H - 1 + qx + 2 * j + i, :, here],
                wide[side, H - 1 + qx + 2 * j + i, :, there],
            )
            for i in range(2)
        ]
        for e in range(3):
            left[48 * e : 48 * e + 48, j * 128 : j * 128 + 128] = jnp.where(
                slot,
                pltpu.roll(pair[0], lax.rem(turn - e, 128), 1),
                pltpu.roll(pair[1], lax.rem(turn + 64 - e, 128), 1),
            )


def correlate(left, right, qy, row, sums):
    c = lax.dot_general(left[...], right[...], (((1,), (1,)), ((), ())), preferred_element_type=F32)
    column = lax.broadcasted_iota(jnp.int32, (W, 144), 1)
    y = jnp.where(column < 48, column, jnp.where(column < 96, column - 48, column - 96))
    lag = lax.broadcasted_iota(jnp.int32, (W, 144), 0) - y - qy

    def diagonal(values, at):
        return jnp.sum(jnp.where(lag == at, values, 0.0), axis=0, keepdims=True)

    def narrow(values, at):
        return jnp.sum(
            jnp.where(lag[:, :128] == at, values[:, :128], 0.0), axis=0, keepdims=True
        )

    centre = diagonal(c[48:96], 0)
    sums[0, pl.ds(row, 1), :] = centre[:, :128]
    sums[1, pl.ds(row, 1), 0:16] = centre[:, 128:144]
    sums[2, pl.ds(row, 1), :] = narrow(c[48:96], -1)
    sums[3, pl.ds(row, 1), :] = narrow(c[48:96], 1)
    sums[4, pl.ds(row, 1), :] = narrow(c[0:48], 0)
    sums[5, pl.ds(row, 1), :] = narrow(c[96:144], 0)


def velocities(sums, peaks):
    c = lane((64, 128))

    def total(k, low, high):
        return jnp.sum(jnp.where((c >= low) & (c < high), sums[k], 0.0), axis=1, keepdims=True)

    columns = (
        total(0, 0, 48),
        total(0, 48, 96),
        total(0, 96, 128) + total(1, 0, 16),
        total(2, 0, 48),
        total(3, 0, 48),
        total(4, 0, 48),
        total(5, 0, 48),
    )
    table = jnp.zeros((64, 128), F32)
    for k, column in enumerate(columns):
        table = jnp.where(c == k, column, table)
    table = jnp.concatenate([table, table], axis=0).T * float(W) ** -1.5
    centre = table[0:1]
    each = lane((1, 128))
    gap = lax.rem(each, 64) // 16
    scale = jnp.where(gap == 0, 1.0, jnp.where(gap == 1, 0.5, jnp.where(gap == 2, 0.25, 0.125)))
    out = jnp.zeros((8, 128), F32)
    row = lax.broadcasted_iota(jnp.int32, (8, 128), 0)
    for axis in range(3):
        lower, upper = table[1 + 2 * axis : 2 + 2 * axis], table[2 + 2 * axis : 3 + 2 * axis]
        curvature = jnp.maximum(2.0 * centre - upper - lower, 1.0)
        value = (peaks[axis : axis + 1].astype(F32) + 0.5 * (upper - lower) / curvature) * scale
        out = jnp.where(row == axis, value, out)
    return jnp.where(row == 3, 1.0, out)


def kernel(
    frames, meta, velocity_out, tile_out,
    F, wide, planes, left0, left1, right0, right1, sums, hot,
    metas, mine, scalars, keys, vector, vectors, beside, parts, arrived,
    local_sem, xs, xr, cs, cr, hs, hr, ms, mr, ss, ks, kr, vs, vr, bs, br, ps, pr,
):
    tm, s = lax.axis_index("tm"), lax.axis_index("space")
    x, core = tm // 2, lax.rem(tm, 2)
    east = 2 * lax.rem(x + 1, 4) + core
    west = 2 * lax.rem(x + 3, 4) + core
    twin = 2 * x + 1 - core
    tiles = [slice(128 * k, 128 * k + 128) for k in range(3)]

    def local(i):
        return pltpu.make_async_copy(frames.at[i], F.at[i, H : H + W], local_sem.at[i])

    for i in range(2):
        local(i).start()

    barrier = pltpu.get_barrier_semaphore()
    greeted = [(tm, lax.rem(s + o, NS)) for o in range(1, NS)]
    greeted += [(lax.rem(tm + o, NT), s) for o in range(1, NT)]
    greeted += [(twin, lax.rem(s + 1, NS)), (twin, lax.rem(s + NS - 1, NS))]
    for device in greeted:
        pl.semaphore_signal(barrier, inc=1, device_id=device, device_id_type=MESH)
    pl.semaphore_wait(barrier, len(greeted))

    def remote(src, dst, send, recv, device):
        return pltpu.make_async_remote_copy(
            src_ref=src, dst_ref=dst, send_sem=send, recv_sem=recv, device_id=device, device_id_type=MESH
        )

    to_east = jnp.where(x < 2, 0, 1)

    def across(side, k):
        frame = to_east if side == 0 else 1 - to_east
        return remote(
            frames.at[frame, :, :, tiles[k]],
            F.at[3 + side, H : H + W, :, tiles[k]],
            xs.at[side, k],
            xr.at[side, k],
            (east if side == 0 else west, s),
        )

    def over():
        return remote(frames.at[1 - core], F.at[2, H : H + W], cs, cr, (twin, s))

    def halo(source, lead, slot, k, way, device_tm):
        low = lead + W - H if way == 0 else lead
        to = 0 if way == 0 else H + W
        return remote(
            source.at[pl.ds(low, H), :, tiles[k]],
            F.at[slot, to : to + H, :, tiles[k]],
            hs.at[slot, way, k],
            hr.at[slot, way, k],
            (device_tm, s + 1 if way == 0 else s - 1),
        )

    has_next = [s < NS - 1, s > 0]
    has_from = [s > 0, s < NS - 1]

    def start_halo(source, lead, slot, k, device_tm, when=None):
        for way in range(2):
            ok = has_next[way] if when is None else has_next[way] & when

            @pl.when(ok)
            def _(way=way):
                halo(source, lead, slot, k, way, device_tm).start()

    def end_halo(source, lead, slot, k, device_tm, when=None):
        for way in range(2):
            ok = has_next[way] if when is None else has_next[way] & when

            @pl.when(ok)
            def _(way=way):
                halo(source, lead, slot, k, way, device_tm).wait_send()

    def got_halo(slot, k, when=None):
        for way in range(2):
            ok = has_from[way] if when is None else has_from[way] & when

            @pl.when(ok)
            def _(way=way):
                halo(F.at[slot], H, slot, k, way, tm).wait_recv()

    own = [frames.at[0], frames.at[1]]
    for side, device in enumerate((east, west)):
        remote(meta, metas.at[side], ms.at[side], mr.at[side], (device, s)).start()
    for k in (2, 1, 0):
        start_halo(own[1], 0, 1, k, tm)
        for side in range(2):
            across(side, k).start()
    over().start()
    for k in (2, 1, 0):
        start_halo(own[0], 0, 2, k, twin, core == 1)
        start_halo(own[0], 0, 0, k, tm, x == 1)

    @pl.when(s == 0)
    def _():
        for slot in range(5):
            F[slot, 0:H] = jnp.zeros((H, W, 384), BF)

    @pl.when(s == NS - 1)
    def _():
        for slot in range(5):
            F[slot, H + W :] = jnp.zeros((H, W, 384), BF)

    wide[:, :, :, 384:] = jnp.zeros((2, EXT, W, 128), BF)
    for right in (right0, right1):
        right[48:96, 24 * 128 :] = jnp.zeros((W, 128), BF)
        right[96:144, 0:128] = jnp.zeros((W, 128), BF)
    sums[...] = jnp.zeros_like(sums)

    for side in range(2):
        remote(meta, metas.at[side], ms.at[side], mr.at[side], (east, s)).wait()
    gap = lax.rem(lane((8, 128)), 64) // 16
    third = jnp.where(x == 0, metas[1], jnp.where(x == 1, metas[0], meta[...]))
    mine[...] = jnp.where(gap < 2, meta[...], jnp.where(gap == 2, third, metas[0]))
    to_scalars = pltpu.make_async_copy(mine, scalars, ss)
    to_scalars.start()

    def key_copy(o):
        return remote(mine, keys.at[s], ks.at[o - 1], kr.at[o - 1], (tm, lax.rem(s + o, NS)))

    for o in range(1, NS):
        key_copy(o).start()
    keys[s] = mine[...]
    to_scalars.wait()

    def by_x(a, b, c, d):
        return jnp.where(x == 0, a, jnp.where(x == 1, b, jnp.where(x == 2, c, d)))

    firsts = [0, jnp.where(core == 0, 0, 2), by_x(1, 3, 0, 3), by_x(4, 3, 3, 4)]
    seconds = [1, jnp.where(core == 0, 2, 1), by_x(4, 0, 4, 1), by_x(3, 4, 4, 3)]

    def stage(pair, k):
        first, second, side = firsts[pair], seconds[pair], pair % 2

        def put(b, _):
            at = pl.ds(8 * b, 8)
            part = F[first, pl.ds(H + 8 * b, 8), :, tiles[k]]
            planes[side, 0, at, :, tiles[k]] = part
            planes[side, 1, at, :, tiles[k]] = pltpu.roll(part, 64, 2)
            return 0

        lax.fori_loop(0, W // 8, put, 0)

        def fill(b, _):
            at = pl.ds(16 * b, 16)
            wide[side, at, :, tiles[k]] = F[second, at, :, tiles[k]]
            return 0

        lax.fori_loop(0, EXT // 16, fill, 0)

    def stage_own(k):
        if k == 2:
            for i in range(2):
                local(i).wait()
        got_halo(1, k)
        stage(0, k)

    def stage_twin(k):
        if k == 2:
            over().wait_recv()
        got_halo(2, k, core == 0)
        stage(1, k)

    def pass_on(k):
        for side in range(2):
            across(side, k).wait_recv()
        for slot in (3, 4):
            uses = (x == 0) | (x == 3) if slot == 3 else x < 3
            start_halo(F.at[slot], H, slot, k, tm, uses)

    def stage_across(k):
        got_halo(0, k, x == 1)
        got_halo(3, k, (x == 0) | (x == 3))
        got_halo(4, k, x < 3)
        stage(2, k)
        stage(3, k)

    def item(i):
        late = i - 30
        pair = jnp.where(i < 15, 0, jnp.where(i < 30, 1, 2 + lax.rem(late + 30, 2)))
        w = jnp.where(i < 15, 14 - i, jnp.where(i < 30, 29 - i, 14 - (late + 30) // 2 + 15))
        return pair, w

    def prepare(i, left, right):
        pair, w = item(i)
        at = 16 * pair + w
        side = lax.rem(pair, 2)
        prepare_first(planes, side, w, right)
        prepare_second(wide, side, w, scalars[0, at], scalars[2, at], left)

    def finish(i, left, right):
        pair, w = item(i)
        at = 16 * pair + w
        correlate(left, right, scalars[1, at], at, sums)

    stage_own(2)
    prepare(0, left0, right0)
    events = {1: (stage_own, 1), 4: (stage_own, 0), 7: (stage_twin, 2), 8: (stage_twin, 1), 11: (stage_twin, 0)}
    events.update({14: (stage_across, 2), 17: (stage_across, 1), 23: (stage_across, 0)})

    def step(h, _):
        for k, at in PASS_STEPS.items():

            @pl.when(h == at)
            def _(k=k):
                pass_on(k)

        for at, (event, k) in events.items():

            @pl.when(h == at)
            def _(event=event, k=k):
                event(k)

        prepare(2 * h + 1, left1, right1)
        finish(2 * h, left0, right0)
        prepare(lax.min(2 * h + 2, 59), left0, right0)
        finish(2 * h + 1, left1, right1)
        return 0

    for o in range(1, NS):
        key_copy(o).wait()
    for pair in range(NS // 2):
        key = jnp.where(lane((1, 128)) < 64, keys[2 * pair, 3:4], keys[2 * pair + 1, 3:4])
        owner = key // CELLS
        cell = key - owner * CELLS
        there = owner // NS
        row = jnp.where((key >= 0) & (owner - there * NS == s), there * CELLS + cell, -1)

        def put(t, _, pair=pair, row=row):
            number = CELLS * t + lax.broadcasted_iota(jnp.int32, (CELLS, 128), 0)
            hot[pl.ds(pl.multiple_of(CELLS * t, CELLS), CELLS), 128 * pair : 128 * pair + 128] = jnp.where(
                number == row, 1.0, 0.0
            ).astype(BF)
            return 0

        lax.fori_loop(0, NT, put, 0)

    lax.fori_loop(0, 30, step, 0)

    values = velocities(sums, mine[...])
    vector[...] = values

    def vector_copy(o):
        return remote(vector, vectors.at[s], vs.at[o - 1], vr.at[o - 1], (tm, lax.rem(s + o, NS)))

    def vector_beside(side):
        return remote(vector, beside.at[side], bs.at[side], br.at[side], (east if side == 0 else west, s))

    for o in range(1, NS):
        vector_copy(o).start()
    for side in range(2):
        vector_beside(side).start()
    vectors[s] = values
    for o in range(1, NS):
        vector_copy(o).wait_recv()
    rows = jnp.concatenate(
        [
            jnp.where(lane((8, 128)) < 64, vectors[2 * pair], vectors[2 * pair + 1])
            for pair in range(NS // 2)
        ],
        axis=1,
    )
    high = rows.astype(BF).astype(F32)
    middle = (rows - high).astype(BF).astype(F32)
    low = rows - high - middle
    split = jnp.concatenate([high, middle, low, jnp.zeros_like(low)], axis=0).astype(BF)
    cell_sums = lax.dot_general(split, hot[...], (((1,), (1,)), ((), ())), preferred_element_type=F32)
    cell_sums = cell_sums[0:8] + cell_sums[8:16] + cell_sums[16:24]
    for t in range(NT):
        parts[t] = cell_sums[:, CELLS * t : CELLS * t + CELLS]

    def part_copy(o):
        to = lax.rem(tm + o, NT)
        return remote(parts.at[to], arrived.at[tm], ps.at[o - 1], pr.at[o - 1], (to, s))

    for o in range(1, NT):
        part_copy(o).start()
    arrived[tm] = parts[tm]

    for side in range(2):
        vector_beside(side).wait()
    gap = lax.rem(lane((8, 128)), 64) // 16
    third = jnp.where(x == 0, beside[1], jnp.where(x == 1, beside[0], values))
    velocity_out[...] = jnp.where(gap < 2, values, jnp.where(gap == 2, third, beside[1]))

    for o in range(1, NS):
        vector_copy(o).wait_send()
    over().wait_send()
    for k in range(3):
        for side in range(2):
            across(side, k).wait_send()
        end_halo(own[1], 0, 1, k, tm)
        end_halo(own[0], 0, 2, k, twin, core == 1)
        end_halo(own[0], 0, 0, k, tm, x == 1)
        end_halo(F.at[3], H, 3, k, tm, (x == 0) | (x == 3))
        end_halo(F.at[4], H, 4, k, tm, x < 3)

    for o in range(1, NT):
        part_copy(o).wait()
    total = arrived[0]
    for t in range(1, NT):
        total = total + arrived[t]
    tile_out[...] = total / jnp.maximum(total[3:4], 1.0)


def on_device(frames, peak_voxels, owners, tile_cells):
    peaks = jnp.transpose(peak_voxels[:, :, 0, :], (1, 0, 2))
    peaks = jnp.pad(peaks, ((0, 0), (0, 0), (0, 1))).reshape(3, 64)
    key = (owners[:, 0] * CELLS + tile_cells).reshape(4, NWIN)
    key = jnp.pad(key, ((0, 0), (0, 1)), constant_values=-1).reshape(1, 64)
    meta = jnp.pad(jnp.concatenate([peaks, key], axis=0), ((0, 4), (0, 0)))
    meta = jnp.concatenate([meta, meta], axis=1)
    dma = pltpu.SemaphoreType.DMA
    vmem = pltpu.VMEM
    velocity, tile = pl.pallas_call(
        kernel,
        out_shape=[jax.ShapeDtypeStruct((8, 128), F32)] * 2,
        in_specs=[pl.BlockSpec(memory_space=pltpu.HBM), pl.BlockSpec(memory_space=vmem)],
        out_specs=[pl.BlockSpec(memory_space=vmem)] * 2,
        scratch_shapes=[
            vmem((5, EXT, W, 384), BF),
            vmem((2, EXT, W, 512), BF),
            vmem((2, 2, W, W, 384), BF),
            vmem((144, DEPTH), BF),
            vmem((144, DEPTH), BF),
            vmem((144, DEPTH), BF),
            vmem((144, DEPTH), BF),
            vmem((6, 64, 128), F32),
            vmem((NT * CELLS, NS * 64), BF),
            vmem((2, 8, 128), jnp.int32),
            vmem((8, 128), jnp.int32),
            pltpu.SMEM((8, 128), jnp.int32),
            vmem((NS, 8, 128), jnp.int32),
            vmem((8, 128), F32),
            vmem((NS, 8, 128), F32),
            vmem((2, 8, 128), F32),
            vmem((NT, 8, 128), F32),
            vmem((NT, 8, 128), F32),
            dma((2,)),
            dma((2, 3)),
            dma((2, 3)),
            dma,
            dma,
            dma((5, 2, 3)),
            dma((5, 2, 3)),
            dma((2,)),
            dma((2,)),
            dma,
            dma((NS - 1,)),
            dma((NS - 1,)),
            dma((NS - 1,)),
            dma((NS - 1,)),
            dma((2,)),
            dma((2,)),
            dma((NT - 1,)),
            dma((NT - 1,)),
        ],
        compiler_params=pltpu.CompilerParams(
            collective_id=0, has_side_effects=True, vmem_limit_bytes=56 * 2**20
        ),
    )(frames, meta)
    velocity = velocity[:3, :64].reshape(3, 4, 16)[:, :, :NWIN]
    return jnp.transpose(velocity, (1, 0, 2))[:, :, None, :], tile[:3]


def solution(mesh):
    placed = (
        P("tm", "space", None, None),
        P(None, None, "tm", "space"),
        P(("tm", "space"), None),
        P(("tm", "space")),
    )
    return jax.shard_map(
        on_device,
        mesh=mesh,
        in_specs=placed,
        out_specs=(P(None, None, "tm", "space"), P(None, ("tm", "space"))),
        check_vma=False,
    )
```

```python
import functools

import jax
import jax.numpy as jnp
from jax import lax
from jax.experimental import pallas as pl
from jax.experimental.pallas import tpu as pltpu
from jax.sharding import PartitionSpec as P

W = 48
H = 16
S = 24
NWIN = 15
CELLS = 128
NS = 16
NT = 8
EXT = W + 2 * H
DEPTH = 25 * 128
BF = jnp.bfloat16
F32 = jnp.float32
MESH = pl.DeviceIdType.MESH

PASS_STEPS = {2: 9, 1: 14, 0: 20}


def lane(shape):
    return lax.broadcasted_iota(jnp.int32, shape, len(shape) - 1)


def prepare_first(planes, side, w, right):
    start = S * w
    tile = start // 128
    offset = start - 128 * tile
    here = pl.ds(pl.multiple_of(128 * tile, 128), 128)
    there = pl.ds(pl.multiple_of(128 * lax.min(tile + 1, 2), 128), 128)
    c = lane((1, 1, 128))
    d = jnp.where(c >= 64, c - 64, c + 64)
    keep = [((v >= offset) & (v < offset + W), v + 128 < offset + W) for v in (c, d)]
    zero = jnp.zeros((2, W, 128), BF)
    previous = None
    for j in range(24):
        low, high = [
            jnp.where(
                keep[r][0],
                planes[side, r, 2 * j : 2 * j + 2, :, here],
                jnp.where(keep[r][1], planes[side, r, 2 * j : 2 * j + 2, :, there], zero),
            )
            for r in range(2)
        ]
        even = low[0] + high[1]
        right[48:96, j * 128 : j * 128 + 128] = even
        right[96:144, j * 128 + 128 : j * 128 + 256] = even
        right[0:48, j * 128 : j * 128 + 128] = high[0] if previous is None else high[0] + previous
        previous = low[1]
    right[0:48, 24 * 128 :] = previous


def prepare_second(wide, side, w, qx, qz, left):
    start = S * w
    base = start - 128 * (start // 128)
    tile = (start + 112) // 128
    offset = start + qz - 1 - 128 * (tile - 1)
    here = pl.ds(pl.multiple_of(128 * lax.rem(tile + 3, 4), 128), 128)
    there = pl.ds(pl.multiple_of(128 * tile, 128), 128)
    c = lane((1, 128))
    d = jnp.where(c >= 64, c - 64, c + 64)
    first, first_turned = c >= offset, d >= offset
    slot = lax.rem(c + 256 - offset, 128) < 64
    turn = base - offset + 512
    for j in range(25):
        x = H - 1 + qx + 2 * j
        even = jnp.where(first, wide[side, 0, x, :, here], wide[side, 0, x, :, there])
        odd = jnp.where(first_turned, wide[side, 1, x + 1, :, here], wide[side, 1, x + 1, :, there])
        pair = jnp.where(slot, even, odd)
        for e in range(3):
            left[48 * e : 48 * e + 48, j * 128 : j * 128 + 128] = pltpu.roll(
                pair, lax.rem(turn - e, 128), 1
            )


def correlate(left, right, qy, row, sums):
    c = lax.dot_general(left[...], right[...], (((1,), (1,)), ((), ())), preferred_element_type=F32)
    column = lax.broadcasted_iota(jnp.int32, (W, 144), 1)
    y = jnp.where(column < 48, column, jnp.where(column < 96, column - 48, column - 96))
    lag = lax.broadcasted_iota(jnp.int32, (W, 144), 0) - y - qy

    def diagonal(values, at):
        return jnp.sum(jnp.where(lag == at, values, 0.0), axis=0, keepdims=True)

    def narrow(values, at):
        return jnp.sum(
            jnp.where(lag[:, :128] == at, values[:, :128], 0.0), axis=0, keepdims=True
        )

    centre = diagonal(c[48:96], 0)
    sums[0, pl.ds(row, 1), :] = centre[:, :128]
    sums[1, pl.ds(row, 1), 0:16] = centre[:, 128:144]
    sums[2, pl.ds(row, 1), :] = narrow(c[48:96], -1)
    sums[3, pl.ds(row, 1), :] = narrow(c[48:96], 1)
    sums[4, pl.ds(row, 1), :] = narrow(c[0:48], 0)
    sums[5, pl.ds(row, 1), :] = narrow(c[96:144], 0)


def velocities(sums, peaks):
    c = lane((64, 128))

    def total(k, low, high):
        return jnp.sum(jnp.where((c >= low) & (c < high), sums[k], 0.0), axis=1, keepdims=True)

    columns = (
        total(0, 0, 48),
        total(0, 48, 96),
        total(0, 96, 128) + total(1, 0, 16),
        total(2, 0, 48),
        total(3, 0, 48),
        total(4, 0, 48),
        total(5, 0, 48),
    )
    table = jnp.zeros((64, 128), F32)
    for k, column in enumerate(columns):
        table = jnp.where(c == k, column, table)
    table = jnp.concatenate([table, table], axis=0).T * float(W) ** -1.5
    centre = table[0:1]
    each = lane((1, 128))
    gap = lax.rem(each, 64) // 16
    scale = jnp.where(gap == 0, 1.0, jnp.where(gap == 1, 0.5, jnp.where(gap == 2, 0.25, 0.125)))
    out = jnp.zeros((8, 128), F32)
    row = lax.broadcasted_iota(jnp.int32, (8, 128), 0)
    for axis in range(3):
        lower, upper = table[1 + 2 * axis : 2 + 2 * axis], table[2 + 2 * axis : 3 + 2 * axis]
        curvature = jnp.maximum(2.0 * centre - upper - lower, 1.0)
        value = (peaks[axis : axis + 1].astype(F32) + 0.5 * (upper - lower) / curvature) * scale
        out = jnp.where(row == axis, value, out)
    return jnp.where(row == 3, 1.0, out)


def kernel(
    frames, meta, velocity_out, tile_out,
    F, wide, planes, left0, left1, right0, right1, sums, hot,
    metas, mine, scalars, keys, vector, vectors, beside, parts, arrived,
    local_sem, xs, xr, cs, cr, hs, hr, ms, mr, ss, ks, kr, vs, vr, bs, br, ps, pr,
):
    tm, s = lax.axis_index("tm"), lax.axis_index("space")
    x, core = tm // 2, lax.rem(tm, 2)
    east = 2 * lax.rem(x + 1, 4) + core
    west = 2 * lax.rem(x + 3, 4) + core
    twin = 2 * x + 1 - core
    tiles = [slice(128 * k, 128 * k + 128) for k in range(3)]

    def local(i):
        return pltpu.make_async_copy(frames.at[i], F.at[i, H : H + W], local_sem.at[i])

    for i in range(2):
        local(i).start()
    pltpu.make_async_copy(meta, scalars, ss).start()

    barrier = pltpu.get_barrier_semaphore()
    greeted = [(tm, lax.rem(s + o, NS)) for o in range(1, NS)]
    greeted += [(lax.rem(tm + o, NT), s) for o in range(1, NT)]
    greeted += [(twin, lax.rem(s + 1, NS)), (twin, lax.rem(s + NS - 1, NS))]
    for device in greeted:
        pl.semaphore_signal(barrier, inc=1, device_id=device, device_id_type=MESH)
    pl.semaphore_wait(barrier, len(greeted))

    def remote(src, dst, send, recv, device):
        return pltpu.make_async_remote_copy(
            src_ref=src, dst_ref=dst, send_sem=send, recv_sem=recv, device_id=device, device_id_type=MESH
        )

    to_east = jnp.where(x < 2, 0, 1)

    def across(side, k):
        frame = to_east if side == 0 else 1 - to_east
        return remote(
            frames.at[frame, :, :, tiles[k]],
            F.at[3 + side, H : H + W, :, tiles[k]],
            xs.at[side, k],
            xr.at[side, k],
            (east if side == 0 else west, s),
        )

    def over():
        return remote(frames.at[1 - core], F.at[2, H : H + W], cs, cr, (twin, s))

    def halo(source, lead, slot, k, way, device_tm):
        low = lead + W - H if way == 0 else lead
        to = 0 if way == 0 else H + W
        return remote(
            source.at[pl.ds(low, H), :, tiles[k]],
            F.at[slot, to : to + H, :, tiles[k]],
            hs.at[slot, way, k],
            hr.at[slot, way, k],
            (device_tm, s + 1 if way == 0 else s - 1),
        )

    has_next = [s < NS - 1, s > 0]
    has_from = [s > 0, s < NS - 1]

    def start_halo(source, lead, slot, k, device_tm, when=None):
        for way in range(2):
            ok = has_next[way] if when is None else has_next[way] & when

            @pl.when(ok)
            def _(way=way):
                halo(source, lead, slot, k, way, device_tm).start()

    def end_halo(source, lead, slot, k, device_tm, when=None):
        for way in range(2):
            ok = has_next[way] if when is None else has_next[way] & when

            @pl.when(ok)
            def _(way=way):
                halo(source, lead, slot, k, way, device_tm).wait_send()

    def got_halo(slot, k, when=None):
        for way in range(2):
            ok = has_from[way] if when is None else has_from[way] & when

            @pl.when(ok)
            def _(way=way):
                halo(F.at[slot], H, slot, k, way, tm).wait_recv()

    own = [frames.at[0], frames.at[1]]

    def meta_copy(side):
        return remote(meta, metas.at[side], ms.at[side], mr.at[side], (east if side == 0 else west, s))

    start_halo(own[1], 0, 1, 2, tm)
    for k in (2, 1, 0):
        for side in range(2):
            across(side, k).start()
    over().start()
    for side in range(2):
        meta_copy(side).start()

    @pl.when(s == 0)
    def _():
        for slot in range(5):
            F[slot, 0:H] = jnp.zeros((H, W, 384), BF)

    @pl.when(s == NS - 1)
    def _():
        for slot in range(5):
            F[slot, H + W :] = jnp.zeros((H, W, 384), BF)

    wide[:, :, :, :, 384:] = jnp.zeros((2, 2, EXT, W, 128), BF)
    for right in (right0, right1):
        right[48:96, 24 * 128 :] = jnp.zeros((W, 128), BF)
        right[96:144, 0:128] = jnp.zeros((W, 128), BF)
    sums[...] = jnp.zeros_like(sums)

    end_halo(own[1], 0, 1, 2, tm)
    for k in (1, 0):
        start_halo(own[1], 0, 1, k, tm)

    def key_copy(o):
        return remote(mine, keys.at[s], ks.at[o - 1], kr.at[o - 1], (tm, lax.rem(s + o, NS)))

    def share_keys():
        for side in range(2):
            meta_copy(side).wait()
        gap = lax.rem(lane((8, 128)), 64) // 16
        third = jnp.where(x == 0, metas[1], jnp.where(x == 1, metas[0], meta[...]))
        mine[...] = jnp.where(gap < 2, meta[...], jnp.where(gap == 2, third, metas[0]))
        to_scalars = pltpu.make_async_copy(mine, scalars, ss)
        to_scalars.start()
        for o in range(1, NS):
            key_copy(o).start()
        keys[s] = mine[...]
        to_scalars.wait()

    def by_x(a, b, c, d):
        return jnp.where(x == 0, a, jnp.where(x == 1, b, jnp.where(x == 2, c, d)))

    firsts = [0, jnp.where(core == 0, 0, 2), by_x(1, 3, 0, 3), by_x(4, 3, 3, 4)]
    seconds = [1, jnp.where(core == 0, 2, 1), by_x(4, 0, 4, 1), by_x(3, 4, 4, 3)]

    def mark_cells():
        for o in range(1, NS):
            key_copy(o).wait()
        for pair in range(NS // 2):
            key = jnp.where(lane((1, 128)) < 64, keys[2 * pair, 3:4], keys[2 * pair + 1, 3:4])
            owner = key // CELLS
            cell = key - owner * CELLS
            there = owner // NS
            row = jnp.where((key >= 0) & (owner - there * NS == s), there * CELLS + cell, -1)

            def put(t, _, pair=pair, row=row):
                number = CELLS * t + lax.broadcasted_iota(jnp.int32, (CELLS, 128), 0)
                hot[pl.ds(pl.multiple_of(CELLS * t, CELLS), CELLS), 128 * pair : 128 * pair + 128] = jnp.where(
                    number == row, 1.0, 0.0
                ).astype(BF)
                return 0

            lax.fori_loop(0, NT, put, 0)

    def stage(pair, k):
        first, second, side = firsts[3], seconds[3], lax.rem(pair, 2)
        for p in range(3):
            first = jnp.where(pair == p, firsts[p], first)
            second = jnp.where(pair == p, seconds[p], second)
        at = pl.ds(pl.multiple_of(128 * k, 128), 128)
        for b in range(0, W, 8):
            part = F[first, H + b : H + b + 8, :, at]
            planes[side, 0, b : b + 8, :, at] = part
            planes[side, 1, b : b + 8, :, at] = pltpu.roll(part, 64, 2)
        for b in range(0, EXT, 8):
            part = F[second, b : b + 8, :, at]
            wide[side, 0, b : b + 8, :, at] = part
            wide[side, 1, b : b + 8, :, at] = pltpu.roll(part, 64, 2)

    def pass_on(k):
        for side in range(2):
            across(side, k).wait_recv()
        start_halo(own[0], 0, 0, k, tm, x == 1)
        for slot in (3, 4):
            uses = (x == 0) | (x == 3) if slot == 3 else x < 3
            start_halo(F.at[slot], H, slot, k, tm, uses)

    def twin_halos():
        for k in (1, 0):
            end_halo(own[1], 0, 1, k, tm)
        for k in (2, 1, 0):
            start_halo(own[0], 0, 2, k, twin, core == 1)

    def got_twin(k):
        if k == 2:
            over().wait_recv()
        got_halo(2, k, core == 0)

    def got_across(k):
        got_halo(0, k, x == 1)
        got_halo(3, k, (x == 0) | (x == 3))
        got_halo(4, k, x < 3)

    def item(i):
        late = i - 30
        pair = jnp.where(i < 15, 0, jnp.where(i < 30, 1, 2 + lax.rem(late + 30, 2)))
        w = jnp.where(i < 15, 14 - i, jnp.where(i < 30, 29 - i, 14 - (late + 30) // 2 + 15))
        return pair, w

    def prepare(i, left, right):
        pair, w = item(i)
        at = 16 * pair + w
        side = lax.rem(pair, 2)
        prepare_first(planes, side, w, right)
        prepare_second(wide, side, w, scalars[0, at], scalars[2, at], left)

    def finish(i, left, right):
        pair, w = item(i)
        at = 16 * pair + w
        correlate(left, right, scalars[1, at], at, sums)

    for i in range(2):
        local(i).wait()
    got_halo(1, 2)
    pltpu.make_async_copy(meta, scalars, ss).wait()
    stage(0, 2)
    prepare(0, left0, right0)
    events = [
        (1, functools.partial(got_halo, 1, 1)),
        (2, share_keys),
        (3, twin_halos),
        (4, functools.partial(got_halo, 1, 0)),
        (5, mark_cells),
        (7, functools.partial(got_twin, 2)),
        (8, functools.partial(got_twin, 1)),
        (11, functools.partial(got_twin, 0)),
    ]
    events += [(at, functools.partial(pass_on, k)) for k, at in PASS_STEPS.items()]
    events += [(at, functools.partial(got_across, k)) for k, at in ((2, 14), (1, 17), (0, 23))]

    def step(h, _):
        for at, event in events:
            pl.when(h == at)(event)

        @pl.when((h == 1) | (h == 4) | (h == 7) | (h == 8) | (h == 11))
        def _():
            stage(jnp.where(h < 7, 0, 1), jnp.where(h == 7, 2, jnp.where((h == 1) | (h == 8), 1, 0)))

        @pl.when((h == 14) | (h == 17) | (h == 23))
        def _():
            def both(pair, _):
                stage(pair, jnp.where(h == 14, 2, jnp.where(h == 17, 1, 0)))
                return 0

            lax.fori_loop(2, 4, both, 0)

        prepare(2 * h + 1, left1, right1)
        finish(2 * h, left0, right0)
        prepare(lax.min(2 * h + 2, 59), left0, right0)
        finish(2 * h + 1, left1, right1)
        return 0

    lax.fori_loop(0, 30, step, 0)

    values = velocities(sums, mine[...])
    vector[...] = values

    def vector_copy(o):
        return remote(vector, vectors.at[s], vs.at[o - 1], vr.at[o - 1], (tm, lax.rem(s + o, NS)))

    def vector_beside(side):
        return remote(vector, beside.at[side], bs.at[side], br.at[side], (east if side == 0 else west, s))

    for o in range(1, NS):
        vector_copy(o).start()
    for side in range(2):
        vector_beside(side).start()
    vectors[s] = values
    for o in range(1, NS):
        vector_copy(o).wait_recv()
    rows = jnp.concatenate(
        [
            jnp.where(lane((8, 128)) < 64, vectors[2 * pair], vectors[2 * pair + 1])
            for pair in range(NS // 2)
        ],
        axis=1,
    )
    high = rows.astype(BF).astype(F32)
    middle = (rows - high).astype(BF).astype(F32)
    low = rows - high - middle
    split = jnp.concatenate([high, middle, low, jnp.zeros_like(low)], axis=0).astype(BF)
    cell_sums = lax.dot_general(split, hot[...], (((1,), (1,)), ((), ())), preferred_element_type=F32)
    cell_sums = cell_sums[0:8] + cell_sums[8:16] + cell_sums[16:24]
    for t in range(NT):
        parts[t] = cell_sums[:, CELLS * t : CELLS * t + CELLS]

    def part_copy(o):
        to = lax.rem(tm + o, NT)
        return remote(parts.at[to], arrived.at[tm], ps.at[o - 1], pr.at[o - 1], (to, s))

    for o in range(1, NT):
        part_copy(o).start()
    arrived[tm] = parts[tm]

    for side in range(2):
        vector_beside(side).wait()
    gap = lax.rem(lane((8, 128)), 64) // 16
    third = jnp.where(x == 0, beside[1], jnp.where(x == 1, beside[0], values))
    listed = jnp.where(gap < 2, values, jnp.where(gap == 2, third, beside[1]))
    for a in range(4):
        for i in range(3):
            velocity_out[a, i] = pltpu.roll(listed, 128 - 16 * a, 1)[i : i + 1, :NWIN] if a else listed[i : i + 1, :NWIN]

    for o in range(1, NS):
        vector_copy(o).wait_send()
    over().wait_send()
    for k in range(3):
        for side in range(2):
            across(side, k).wait_send()
        end_halo(own[0], 0, 2, k, twin, core == 1)
        end_halo(own[0], 0, 0, k, tm, x == 1)
        end_halo(F.at[3], H, 3, k, tm, (x == 0) | (x == 3))
        end_halo(F.at[4], H, 4, k, tm, x < 3)

    for o in range(1, NT):
        part_copy(o).wait()
    total = arrived[0]
    for t in range(1, NT):
        total = total + arrived[t]
    tile_out[...] = total[0:3] / jnp.maximum(total[3:4], 1.0)


def on_device(frames, peak_voxels, owners, tile_cells):
    peaks = jnp.transpose(peak_voxels[:, :, 0, :], (1, 0, 2))
    peaks = jnp.pad(peaks, ((0, 0), (0, 0), (0, 1))).reshape(3, 64)
    key = (owners[:, 0] * CELLS + tile_cells).reshape(4, NWIN)
    key = jnp.pad(key, ((0, 0), (0, 1)), constant_values=-1).reshape(1, 64)
    meta = jnp.pad(jnp.concatenate([peaks, key], axis=0), ((0, 4), (0, 0)))
    meta = jnp.concatenate([meta, meta], axis=1)
    dma = pltpu.SemaphoreType.DMA
    vmem = pltpu.VMEM
    velocity, tile = pl.pallas_call(
        kernel,
        out_shape=[jax.ShapeDtypeStruct((4, 3, 1, NWIN), F32), jax.ShapeDtypeStruct((3, CELLS), F32)],
        in_specs=[pl.BlockSpec(memory_space=pltpu.HBM), pl.BlockSpec(memory_space=vmem)],
        out_specs=[pl.BlockSpec(memory_space=vmem)] * 2,
        scratch_shapes=[
            vmem((5, EXT, W, 384), BF),
            vmem((2, 2, EXT, W, 512), BF),
            vmem((2, 2, W, W, 384), BF),
            vmem((144, DEPTH), BF),
            vmem((144, DEPTH), BF),
            vmem((144, DEPTH), BF),
            vmem((144, DEPTH), BF),
            vmem((6, 64, 128), F32),
            vmem((NT * CELLS, NS * 64), BF),
            vmem((2, 8, 128), jnp.int32),
            vmem((8, 128), jnp.int32),
            pltpu.SMEM((8, 128), jnp.int32),
            vmem((NS, 8, 128), jnp.int32),
            vmem((8, 128), F32),
            vmem((NS, 8, 128), F32),
            vmem((2, 8, 128), F32),
            vmem((NT, 8, 128), F32),
            vmem((NT, 8, 128), F32),
            dma((2,)),
            dma((2, 3)),
            dma((2, 3)),
            dma,
            dma,
            dma((5, 2, 3)),
            dma((5, 2, 3)),
            dma((2,)),
            dma((2,)),
            dma,
            dma((NS - 1,)),
            dma((NS - 1,)),
            dma((NS - 1,)),
            dma((NS - 1,)),
            dma((2,)),
            dma((2,)),
            dma((NT - 1,)),
            dma((NT - 1,)),
        ],
        compiler_params=pltpu.CompilerParams(
            collective_id=0, has_side_effects=True, vmem_limit_bytes=56 * 2**20
        ),
    )(frames, meta)
    return velocity, tile


def solution(mesh):
    placed = (
        P("tm", "space", None, None),
        P(None, None, "tm", "space"),
        P(("tm", "space"), None),
        P(("tm", "space")),
    )
    return jax.shard_map(
        on_device,
        mesh=mesh,
        in_specs=placed,
        out_specs=(P(None, None, "tm", "space"), P(None, ("tm", "space"))),
        check_vma=False,
    )
```

```python
import functools

import jax
import jax.numpy as jnp
from jax import lax
from jax.experimental import pallas as pl
from jax.experimental.pallas import tpu as pltpu
from jax.sharding import PartitionSpec as P

W = 48
H = 16
S = 24
NWIN = 15
CELLS = 128
NS = 16
NT = 8
EXT = W + 2 * H
DEPTH = 25 * 128
BF = jnp.bfloat16
F32 = jnp.float32
MESH = pl.DeviceIdType.MESH

PASS_STEPS = {2: 6, 1: 10, 0: 15}
SEND_STEPS = (1, 5, 9, 12)


def lane(shape):
    return lax.broadcasted_iota(jnp.int32, shape, len(shape) - 1)


def prepare_first(planes, side, w, right):
    start = S * w
    tile = start // 128
    offset = start - 128 * tile
    here = pl.ds(pl.multiple_of(128 * tile, 128), 128)
    there = pl.ds(pl.multiple_of(128 * lax.min(tile + 1, 2), 128), 128)
    c = lane((1, 1, 128))
    d = jnp.where(c >= 64, c - 64, c + 64)
    keep = [((v >= offset) & (v < offset + W), v + 128 < offset + W) for v in (c, d)]
    zero = jnp.zeros((2, W, 128), BF)
    previous = None
    for j in range(24):
        low, high = [
            jnp.where(
                keep[r][0],
                planes[side, r, 2 * j : 2 * j + 2, :, here],
                jnp.where(keep[r][1], planes[side, r, 2 * j : 2 * j + 2, :, there], zero),
            )
            for r in range(2)
        ]
        even = low[0] + high[1]
        right[48:96, j * 128 : j * 128 + 128] = even
        right[96:144, j * 128 + 128 : j * 128 + 256] = even
        right[0:48, j * 128 : j * 128 + 128] = high[0] if previous is None else high[0] + previous
        previous = low[1]
    right[0:48, 24 * 128 :] = previous


def prepare_second(wide, side, w, qx, qz, left):
    start = S * w
    base = start - 128 * (start // 128)
    tile = (start + 112) // 128
    offset = start + qz - 1 - 128 * (tile - 1)
    here = pl.ds(pl.multiple_of(128 * lax.rem(tile + 3, 4), 128), 128)
    there = pl.ds(pl.multiple_of(128 * tile, 128), 128)
    c = lane((1, 128))
    d = jnp.where(c >= 64, c - 64, c + 64)
    first, first_turned = c >= offset, d >= offset
    slot = lax.rem(c + 256 - offset, 128) < 64
    turn = base - offset + 512
    for j in range(25):
        x = H - 1 + qx + 2 * j
        even = jnp.where(first, wide[side, 0, x, :, here], wide[side, 0, x, :, there])
        odd = jnp.where(first_turned, wide[side, 1, x + 1, :, here], wide[side, 1, x + 1, :, there])
        pair = jnp.where(slot, even, odd)
        for e in range(3):
            left[48 * e : 48 * e + 48, j * 128 : j * 128 + 128] = pltpu.roll(
                pair, lax.rem(turn - e, 128), 1
            )


def correlate(left, right, qy, row, sums):
    c = lax.dot_general(left[...], right[...], (((1,), (1,)), ((), ())), preferred_element_type=F32)
    column = lax.broadcasted_iota(jnp.int32, (W, 144), 1)
    y = jnp.where(column < 48, column, jnp.where(column < 96, column - 48, column - 96))
    lag = lax.broadcasted_iota(jnp.int32, (W, 144), 0) - y - qy

    def diagonal(values, at):
        return jnp.sum(jnp.where(lag == at, values, 0.0), axis=0, keepdims=True)

    def narrow(values, at):
        return jnp.sum(
            jnp.where(lag[:, :128] == at, values[:, :128], 0.0), axis=0, keepdims=True
        )

    centre = diagonal(c[48:96], 0)
    sums[0, pl.ds(row, 1), :] = centre[:, :128]
    sums[1, pl.ds(row, 1), 0:16] = centre[:, 128:144]
    sums[2, pl.ds(row, 1), :] = narrow(c[48:96], -1)
    sums[3, pl.ds(row, 1), :] = narrow(c[48:96], 1)
    sums[4, pl.ds(row, 1), :] = narrow(c[0:48], 0)
    sums[5, pl.ds(row, 1), :] = narrow(c[96:144], 0)


def velocities(sums, peaks):
    c = lane((64, 128))

    def total(k, low, high):
        return jnp.sum(jnp.where((c >= low) & (c < high), sums[k], 0.0), axis=1, keepdims=True)

    columns = (
        total(0, 0, 48),
        total(0, 48, 96),
        total(0, 96, 128) + total(1, 0, 16),
        total(2, 0, 48),
        total(3, 0, 48),
        total(4, 0, 48),
        total(5, 0, 48),
    )
    table = jnp.zeros((64, 128), F32)
    for k, column in enumerate(columns):
        table = jnp.where(c == k, column, table)
    table = jnp.concatenate([table, table], axis=0).T * float(W) ** -1.5
    centre = table[0:1]
    each = lane((1, 128))
    gap = lax.rem(each, 64) // 16
    scale = jnp.where(gap == 0, 1.0, jnp.where(gap == 1, 0.5, jnp.where(gap == 2, 0.25, 0.125)))
    out = jnp.zeros((8, 128), F32)
    row = lax.broadcasted_iota(jnp.int32, (8, 128), 0)
    for axis in range(3):
        lower, upper = table[1 + 2 * axis : 2 + 2 * axis], table[2 + 2 * axis : 3 + 2 * axis]
        curvature = jnp.maximum(2.0 * centre - upper - lower, 1.0)
        value = (peaks[axis : axis + 1].astype(F32) + 0.5 * (upper - lower) / curvature) * scale
        out = jnp.where(row == axis, value, out)
    return jnp.where(row == 3, 1.0, out)


def kernel(
    frames, meta, velocity_out, tile_out,
    F, wide, planes, left0, left1, right0, right1, sums, hot,
    metas, mine, scalars, keys, vector, vectors, beside, parts, arrived,
    local_sem, xs, xr, cs, cr, hs, hr, ms, mr, ss, ks, kr, vs, vr, bs, br, ps, pr,
):
    tm, s = lax.axis_index("tm"), lax.axis_index("space")
    x, core = tm // 2, lax.rem(tm, 2)
    east = 2 * lax.rem(x + 1, 4) + core
    west = 2 * lax.rem(x + 3, 4) + core
    twin = 2 * x + 1 - core
    tiles = [slice(128 * k, 128 * k + 128) for k in range(3)]

    def local(i):
        return pltpu.make_async_copy(frames.at[i], F.at[i, H : H + W], local_sem.at[i])

    for i in range(2):
        local(i).start()
    pltpu.make_async_copy(meta, scalars, ss).start()

    barrier = pltpu.get_barrier_semaphore()
    greeted = [(tm, lax.rem(s + o, NS)) for o in range(1, NS)]
    greeted += [(lax.rem(tm + o, NT), s) for o in range(1, NT)]
    greeted += [(twin, lax.rem(s + 1, NS)), (twin, lax.rem(s + NS - 1, NS))]
    for device in greeted:
        pl.semaphore_signal(barrier, inc=1, device_id=device, device_id_type=MESH)
    pl.semaphore_wait(barrier, len(greeted))

    def remote(src, dst, send, recv, device):
        return pltpu.make_async_remote_copy(
            src_ref=src, dst_ref=dst, send_sem=send, recv_sem=recv, device_id=device, device_id_type=MESH
        )

    to_east = jnp.where(x < 2, 0, 1)

    def across(side, k, part):
        frame = to_east if side == 0 else 1 - to_east
        low = (0, W - H, H)[part]
        return remote(
            frames.at[frame, low : low + H, :, tiles[k]],
            F.at[3 + side, H + low : H + low + H, :, tiles[k]],
            xs.at[side, k, part],
            xr.at[side, k, part],
            (east if side == 0 else west, s),
        )

    def each_across(ks, parts, act):
        for k in ks:
            for part in parts:
                for side in range(2):
                    act(across(side, k, part))

    def begin(copy):
        copy.start()

    def sent(copy):
        copy.wait_send()

    def received(copy):
        copy.wait_recv()

    outer, inner = (0, 1), (2,)

    def next_across(past, past_parts, ks, parts):
        each_across(past, past_parts, sent)
        each_across(ks, parts, begin)

    sends = (
        ((2,), outer, (1,), outer),
        ((1,), outer, (0,), outer),
        ((0,), outer, (2,), inner),
        ((2,), inner, (1, 0), inner),
    )

    def over():
        return remote(frames.at[1 - core], F.at[2, H : H + W], cs, cr, (twin, s))

    def halo(source, lead, slot, k, way, device_tm):
        low = lead + W - H if way == 0 else lead
        to = 0 if way == 0 else H + W
        return remote(
            source.at[pl.ds(low, H), :, tiles[k]],
            F.at[slot, to : to + H, :, tiles[k]],
            hs.at[slot, way, k],
            hr.at[slot, way, k],
            (device_tm, s + 1 if way == 0 else s - 1),
        )

    has_next = [s < NS - 1, s > 0]
    has_from = [s > 0, s < NS - 1]

    def start_halo(source, lead, slot, k, device_tm, when=None):
        for way in range(2):
            ok = has_next[way] if when is None else has_next[way] & when

            @pl.when(ok)
            def _(way=way):
                halo(source, lead, slot, k, way, device_tm).start()

    def end_halo(source, lead, slot, k, device_tm, when=None):
        for way in range(2):
            ok = has_next[way] if when is None else has_next[way] & when

            @pl.when(ok)
            def _(way=way):
                halo(source, lead, slot, k, way, device_tm).wait_send()

    def got_halo(slot, k, when=None):
        for way in range(2):
            ok = has_from[way] if when is None else has_from[way] & when

            @pl.when(ok)
            def _(way=way):
                halo(F.at[slot], H, slot, k, way, tm).wait_recv()

    own = [frames.at[0], frames.at[1]]

    def meta_copy(side):
        return remote(meta, metas.at[side], ms.at[side], mr.at[side], (east if side == 0 else west, s))

    start_halo(own[1], 0, 1, 2, tm)
    each_across((2,), outer, begin)
    over().start()
    for side in range(2):
        meta_copy(side).start()

    @pl.when(s == 0)
    def _():
        for slot in range(5):
            F[slot, 0:H] = jnp.zeros((H, W, 384), BF)

    @pl.when(s == NS - 1)
    def _():
        for slot in range(5):
            F[slot, H + W :] = jnp.zeros((H, W, 384), BF)

    wide[:, :, :, :, 384:] = jnp.zeros((2, 2, EXT, W, 128), BF)
    for right in (right0, right1):
        right[48:96, 24 * 128 :] = jnp.zeros((W, 128), BF)
        right[96:144, 0:128] = jnp.zeros((W, 128), BF)
    sums[...] = jnp.zeros_like(sums)

    end_halo(own[1], 0, 1, 2, tm)
    for k in (1, 0):
        start_halo(own[1], 0, 1, k, tm)

    def key_copy(o):
        return remote(mine, keys.at[s], ks.at[o - 1], kr.at[o - 1], (tm, lax.rem(s + o, NS)))

    def share_keys():
        for side in range(2):
            meta_copy(side).wait()
        gap = lax.rem(lane((8, 128)), 64) // 16
        third = jnp.where(x == 0, metas[1], jnp.where(x == 1, metas[0], meta[...]))
        mine[...] = jnp.where(gap < 2, meta[...], jnp.where(gap == 2, third, metas[0]))
        to_scalars = pltpu.make_async_copy(mine, scalars, ss)
        to_scalars.start()
        for o in range(1, NS):
            key_copy(o).start()
        keys[s] = mine[...]
        to_scalars.wait()

    def by_x(a, b, c, d):
        return jnp.where(x == 0, a, jnp.where(x == 1, b, jnp.where(x == 2, c, d)))

    firsts = [0, jnp.where(core == 0, 0, 2), by_x(1, 3, 0, 3), by_x(4, 3, 3, 4)]
    seconds = [1, jnp.where(core == 0, 2, 1), by_x(4, 0, 4, 1), by_x(3, 4, 4, 3)]

    def mark_cells():
        for o in range(1, NS):
            key_copy(o).wait()
        for pair in range(NS // 2):
            key = jnp.where(lane((1, 128)) < 64, keys[2 * pair, 3:4], keys[2 * pair + 1, 3:4])
            owner = key // CELLS
            cell = key - owner * CELLS
            there = owner // NS
            row = jnp.where((key >= 0) & (owner - there * NS == s), there * CELLS + cell, -1)

            def put(t, _, pair=pair, row=row):
                number = CELLS * t + lax.broadcasted_iota(jnp.int32, (CELLS, 128), 0)
                hot[pl.ds(pl.multiple_of(CELLS * t, CELLS), CELLS), 128 * pair : 128 * pair + 128] = jnp.where(
                    number == row, 1.0, 0.0
                ).astype(BF)
                return 0

            lax.fori_loop(0, NT, put, 0)

    def stage(pair, k):
        first, second, side = firsts[3], seconds[3], lax.rem(pair, 2)
        for p in range(3):
            first = jnp.where(pair == p, firsts[p], first)
            second = jnp.where(pair == p, seconds[p], second)
        at = pl.ds(pl.multiple_of(128 * k, 128), 128)
        for b in range(0, W, 8):
            part = F[first, H + b : H + b + 8, :, at]
            planes[side, 0, b : b + 8, :, at] = part
            planes[side, 1, b : b + 8, :, at] = pltpu.roll(part, 64, 2)
        for b in range(0, EXT, 8):
            part = F[second, b : b + 8, :, at]
            wide[side, 0, b : b + 8, :, at] = part
            wide[side, 1, b : b + 8, :, at] = pltpu.roll(part, 64, 2)

    def pass_on(k):
        each_across((k,), outer, received)
        start_halo(own[0], 0, 0, k, tm, x == 1)
        for slot in (3, 4):
            uses = (x == 0) | (x == 3) if slot == 3 else x < 3
            start_halo(F.at[slot], H, slot, k, tm, uses)

    def twin_halos():
        for k in (1, 0):
            end_halo(own[1], 0, 1, k, tm)
        for k in (2, 1, 0):
            start_halo(own[0], 0, 2, k, twin, core == 1)

    def got_twin(k):
        if k == 2:
            over().wait_recv()
        got_halo(2, k, core == 0)

    def got_across(k):
        each_across((k,), inner, received)
        got_halo(0, k, x == 1)
        got_halo(3, k, (x == 0) | (x == 3))
        got_halo(4, k, x < 3)

    def item(i):
        late = i - 30
        pair = jnp.where(i < 15, 0, jnp.where(i < 30, 1, 2 + lax.rem(late + 30, 2)))
        w = jnp.where(i < 15, 14 - i, jnp.where(i < 30, 29 - i, 14 - (late + 30) // 2 + 15))
        return pair, w

    def prepare(i, left, right):
        pair, w = item(i)
        at = 16 * pair + w
        side = lax.rem(pair, 2)
        prepare_first(planes, side, w, right)
        prepare_second(wide, side, w, scalars[0, at], scalars[2, at], left)

    def finish(i, left, right):
        pair, w = item(i)
        at = 16 * pair + w
        correlate(left, right, scalars[1, at], at, sums)

    for i in range(2):
        local(i).wait()
    got_halo(1, 2)
    pltpu.make_async_copy(meta, scalars, ss).wait()
    stage(0, 2)
    prepare(0, left0, right0)
    events = [
        (1, functools.partial(got_halo, 1, 1)),
        (2, share_keys),
        (3, twin_halos),
        (4, functools.partial(got_halo, 1, 0)),
        (5, mark_cells),
        (7, functools.partial(got_twin, 2)),
        (8, functools.partial(got_twin, 1)),
        (11, functools.partial(got_twin, 0)),
    ]
    events += [(at, functools.partial(next_across, *send)) for at, send in zip(SEND_STEPS, sends)]
    events += [(at, functools.partial(pass_on, k)) for k, at in PASS_STEPS.items()]
    events += [(at, functools.partial(got_across, k)) for k, at in ((2, 14), (1, 17), (0, 23))]

    def step(h, _):
        for at, event in events:
            pl.when(h == at)(event)

        @pl.when((h == 1) | (h == 4) | (h == 7) | (h == 8) | (h == 11))
        def _():
            stage(jnp.where(h < 7, 0, 1), jnp.where(h == 7, 2, jnp.where((h == 1) | (h == 8), 1, 0)))

        @pl.when((h == 14) | (h == 17) | (h == 23))
        def _():
            def both(pair, _):
                stage(pair, jnp.where(h == 14, 2, jnp.where(h == 17, 1, 0)))
                return 0

            lax.fori_loop(2, 4, both, 0)

        prepare(2 * h + 1, left1, right1)
        finish(2 * h, left0, right0)
        prepare(lax.min(2 * h + 2, 59), left0, right0)
        finish(2 * h + 1, left1, right1)
        return 0

    lax.fori_loop(0, 30, step, 0)

    values = velocities(sums, mine[...])
    vector[...] = values

    def vector_copy(o):
        return remote(vector, vectors.at[s], vs.at[o - 1], vr.at[o - 1], (tm, lax.rem(s + o, NS)))

    def vector_beside(side):
        return remote(vector, beside.at[side], bs.at[side], br.at[side], (east if side == 0 else west, s))

    for o in range(1, NS):
        vector_copy(o).start()
    for side in range(2):
        vector_beside(side).start()
    vectors[s] = values
    for o in range(1, NS):
        vector_copy(o).wait_recv()
    rows = jnp.concatenate(
        [
            jnp.where(lane((8, 128)) < 64, vectors[2 * pair], vectors[2 * pair + 1])
            for pair in range(NS // 2)
        ],
        axis=1,
    )
    high = rows.astype(BF).astype(F32)
    middle = (rows - high).astype(BF).astype(F32)
    low = rows - high - middle
    split = jnp.concatenate([high, middle, low, jnp.zeros_like(low)], axis=0).astype(BF)
    cell_sums = lax.dot_general(split, hot[...], (((1,), (1,)), ((), ())), preferred_element_type=F32)
    cell_sums = cell_sums[0:8] + cell_sums[8:16] + cell_sums[16:24]
    for t in range(NT):
        parts[t] = cell_sums[:, CELLS * t : CELLS * t + CELLS]

    def part_copy(o):
        to = lax.rem(tm + o, NT)
        return remote(parts.at[to], arrived.at[tm], ps.at[o - 1], pr.at[o - 1], (to, s))

    for o in range(1, NT):
        part_copy(o).start()
    arrived[tm] = parts[tm]

    for side in range(2):
        vector_beside(side).wait()
    gap = lax.rem(lane((8, 128)), 64) // 16
    third = jnp.where(x == 0, beside[1], jnp.where(x == 1, beside[0], values))
    listed = jnp.where(gap < 2, values, jnp.where(gap == 2, third, beside[1]))
    for a in range(4):
        for i in range(3):
            velocity_out[a, i] = pltpu.roll(listed, 128 - 16 * a, 1)[i : i + 1, :NWIN] if a else listed[i : i + 1, :NWIN]

    for o in range(1, NS):
        vector_copy(o).wait_send()
    over().wait_send()
    each_across((1, 0), inner, sent)
    for k in range(3):
        end_halo(own[0], 0, 2, k, twin, core == 1)
        end_halo(own[0], 0, 0, k, tm, x == 1)
        end_halo(F.at[3], H, 3, k, tm, (x == 0) | (x == 3))
        end_halo(F.at[4], H, 4, k, tm, x < 3)

    for o in range(1, NT):
        part_copy(o).wait()
    total = arrived[0]
    for t in range(1, NT):
        total = total + arrived[t]
    tile_out[...] = total[0:3] / jnp.maximum(total[3:4], 1.0)


def on_device(frames, peak_voxels, owners, tile_cells):
    peaks = jnp.transpose(peak_voxels[:, :, 0, :], (1, 0, 2))
    peaks = jnp.pad(peaks, ((0, 0), (0, 0), (0, 1))).reshape(3, 64)
    key = (owners[:, 0] * CELLS + tile_cells).reshape(4, NWIN)
    key = jnp.pad(key, ((0, 0), (0, 1)), constant_values=-1).reshape(1, 64)
    meta = jnp.pad(jnp.concatenate([peaks, key], axis=0), ((0, 4), (0, 0)))
    meta = jnp.concatenate([meta, meta], axis=1)
    dma = pltpu.SemaphoreType.DMA
    vmem = pltpu.VMEM
    velocity, tile = pl.pallas_call(
        kernel,
        out_shape=[jax.ShapeDtypeStruct((4, 3, 1, NWIN), F32), jax.ShapeDtypeStruct((3, CELLS), F32)],
        in_specs=[pl.BlockSpec(memory_space=pltpu.HBM), pl.BlockSpec(memory_space=vmem)],
        out_specs=[pl.BlockSpec(memory_space=vmem)] * 2,
        scratch_shapes=[
            vmem((5, EXT, W, 384), BF),
            vmem((2, 2, EXT, W, 512), BF),
            vmem((2, 2, W, W, 384), BF),
            vmem((144, DEPTH), BF),
            vmem((144, DEPTH), BF),
            vmem((144, DEPTH), BF),
            vmem((144, DEPTH), BF),
            vmem((6, 64, 128), F32),
            vmem((NT * CELLS, NS * 64), BF),
            vmem((2, 8, 128), jnp.int32),
            vmem((8, 128), jnp.int32),
            pltpu.SMEM((8, 128), jnp.int32),
            vmem((NS, 8, 128), jnp.int32),
            vmem((8, 128), F32),
            vmem((NS, 8, 128), F32),
            vmem((2, 8, 128), F32),
            vmem((NT, 8, 128), F32),
            vmem((NT, 8, 128), F32),
            dma((2,)),
            dma((2, 3, 3)),
            dma((2, 3, 3)),
            dma,
            dma,
            dma((5, 2, 3)),
            dma((5, 2, 3)),
            dma((2,)),
            dma((2,)),
            dma,
            dma((NS - 1,)),
            dma((NS - 1,)),
            dma((NS - 1,)),
            dma((NS - 1,)),
            dma((2,)),
            dma((2,)),
            dma((NT - 1,)),
            dma((NT - 1,)),
        ],
        compiler_params=pltpu.CompilerParams(
            collective_id=0, has_side_effects=True, vmem_limit_bytes=56 * 2**20
        ),
    )(frames, meta)
    return velocity, tile


def solution(mesh):
    placed = (
        P("tm", "space", None, None),
        P(None, None, "tm", "space"),
        P(("tm", "space"), None),
        P(("tm", "space")),
    )
    return jax.shard_map(
        on_device,
        mesh=mesh,
        in_specs=placed,
        out_specs=(P(None, None, "tm", "space"), P(None, ("tm", "space"))),
        check_vma=False,
    )
```

```python
import functools

import jax
import jax.numpy as jnp
from jax import lax
from jax.experimental import pallas as pl
from jax.experimental.pallas import tpu as pltpu
from jax.sharding import PartitionSpec as P

W = 48
H = 16
S = 24
NWIN = 15
CELLS = 128
NS = 16
NT = 8
EXT = W + 2 * H
DEPTH = 25 * 128
BF = jnp.bfloat16
F32 = jnp.float32
MESH = pl.DeviceIdType.MESH

PASS_STEPS = {2: 6, 1: 10, 0: 14}
SEND_STEPS = (2, 6, 10, 13)


def lane(shape):
    return lax.broadcasted_iota(jnp.int32, shape, len(shape) - 1)


def prepare_first(planes, side, w, right):
    start = S * w
    tile = start // 128
    offset = start - 128 * tile
    here = pl.ds(pl.multiple_of(128 * tile, 128), 128)
    there = pl.ds(pl.multiple_of(128 * lax.min(tile + 1, 2), 128), 128)
    c = lane((1, 1, 128))
    d = jnp.where(c >= 64, c - 64, c + 64)
    keep = [((v >= offset) & (v < offset + W), v + 128 < offset + W) for v in (c, d)]
    zero = jnp.zeros((2, W, 128), BF)
    previous = None
    for j in range(24):
        low, high = [
            jnp.where(
                keep[r][0],
                planes[side, r, 2 * j : 2 * j + 2, :, here],
                jnp.where(keep[r][1], planes[side, r, 2 * j : 2 * j + 2, :, there], zero),
            )
            for r in range(2)
        ]
        even = low[0] + high[1]
        right[48:96, j * 128 : j * 128 + 128] = even
        right[96:144, j * 128 + 128 : j * 128 + 256] = even
        right[0:48, j * 128 : j * 128 + 128] = high[0] if previous is None else high[0] + previous
        previous = low[1]
    right[0:48, 24 * 128 :] = previous


def prepare_second(wide, side, w, qx, qz, left):
    start = S * w
    base = start - 128 * (start // 128)
    tile = (start + 112) // 128
    offset = start + qz - 1 - 128 * (tile - 1)
    here = pl.ds(pl.multiple_of(128 * lax.rem(tile + 3, 4), 128), 128)
    there = pl.ds(pl.multiple_of(128 * tile, 128), 128)
    c = lane((1, 128))
    d = jnp.where(c >= 64, c - 64, c + 64)
    first, first_turned = c >= offset, d >= offset
    slot = lax.rem(c + 256 - offset, 128) < 64
    turn = base - offset + 512
    for j in range(25):
        x = H - 1 + qx + 2 * j
        even = jnp.where(first, wide[side, 0, x, :, here], wide[side, 0, x, :, there])
        odd = jnp.where(first_turned, wide[side, 1, x + 1, :, here], wide[side, 1, x + 1, :, there])
        pair = jnp.where(slot, even, odd)
        for e in range(3):
            left[48 * e : 48 * e + 48, j * 128 : j * 128 + 128] = pltpu.roll(
                pair, lax.rem(turn - e, 128), 1
            )


def correlate(left, right, qy, row, sums):
    c = lax.dot_general(left[...], right[...], (((1,), (1,)), ((), ())), preferred_element_type=F32)
    column = lax.broadcasted_iota(jnp.int32, (W, 144), 1)
    y = jnp.where(column < 48, column, jnp.where(column < 96, column - 48, column - 96))
    lag = lax.broadcasted_iota(jnp.int32, (W, 144), 0) - y - qy

    def diagonal(values, at):
        return jnp.sum(jnp.where(lag == at, values, 0.0), axis=0, keepdims=True)

    def narrow(values, at):
        return jnp.sum(
            jnp.where(lag[:, :128] == at, values[:, :128], 0.0), axis=0, keepdims=True
        )

    centre = diagonal(c[48:96], 0)
    sums[0, pl.ds(row, 1), :] = centre[:, :128]
    sums[1, pl.ds(row, 1), 0:16] = centre[:, 128:144]
    sums[2, pl.ds(row, 1), :] = narrow(c[48:96], -1)
    sums[3, pl.ds(row, 1), :] = narrow(c[48:96], 1)
    sums[4, pl.ds(row, 1), :] = narrow(c[0:48], 0)
    sums[5, pl.ds(row, 1), :] = narrow(c[96:144], 0)


def velocities(sums, peaks):
    c = lane((64, 128))

    def total(k, low, high):
        return jnp.sum(jnp.where((c >= low) & (c < high), sums[k], 0.0), axis=1, keepdims=True)

    columns = (
        total(0, 0, 48),
        total(0, 48, 96),
        total(0, 96, 128) + total(1, 0, 16),
        total(2, 0, 48),
        total(3, 0, 48),
        total(4, 0, 48),
        total(5, 0, 48),
    )
    table = jnp.zeros((64, 128), F32)
    for k, column in enumerate(columns):
        table = jnp.where(c == k, column, table)
    table = jnp.concatenate([table, table], axis=0).T * float(W) ** -1.5
    centre = table[0:1]
    each = lane((1, 128))
    gap = lax.rem(each, 64) // 16
    scale = jnp.where(gap == 0, 1.0, jnp.where(gap == 1, 0.5, jnp.where(gap == 2, 0.25, 0.125)))
    out = jnp.zeros((8, 128), F32)
    row = lax.broadcasted_iota(jnp.int32, (8, 128), 0)
    for axis in range(3):
        lower, upper = table[1 + 2 * axis : 2 + 2 * axis], table[2 + 2 * axis : 3 + 2 * axis]
        curvature = jnp.maximum(2.0 * centre - upper - lower, 1.0)
        value = (peaks[axis : axis + 1].astype(F32) + 0.5 * (upper - lower) / curvature) * scale
        out = jnp.where(row == axis, value, out)
    return jnp.where(row == 3, 1.0, out)


def kernel(
    frames, meta, velocity_out, tile_out,
    F, wide, planes, left0, left1, right0, right1, sums, hot,
    metas, mine, scalars, keys, vector, vectors, beside, parts, arrived,
    local_sem, xs, xr, cs, cr, hs, hr, ms, mr, ss, ks, kr, vs, vr, bs, br, ps, pr,
):
    tm, s = lax.axis_index("tm"), lax.axis_index("space")
    x, core = tm // 2, lax.rem(tm, 2)
    east = 2 * lax.rem(x + 1, 4) + core
    west = 2 * lax.rem(x + 3, 4) + core
    twin = 2 * x + 1 - core
    tiles = [slice(128 * k, 128 * k + 128) for k in range(3)]

    def local(i):
        return pltpu.make_async_copy(frames.at[i], F.at[i, H : H + W], local_sem.at[i])

    for i in range(2):
        local(i).start()
    pltpu.make_async_copy(meta, scalars, ss).start()

    barrier = pltpu.get_barrier_semaphore()
    greeted = [(tm, lax.rem(s + o, NS)) for o in range(1, NS)]
    greeted += [(lax.rem(tm + o, NT), s) for o in range(1, NT)]
    greeted += [(twin, lax.rem(s + 1, NS)), (twin, lax.rem(s + NS - 1, NS))]
    for device in greeted:
        pl.semaphore_signal(barrier, inc=1, device_id=device, device_id_type=MESH)
    @pl.when(s == 0)
    def _():
        for slot in range(5):
            F[slot, 0:H] = jnp.zeros((H, W, 384), BF)

    @pl.when(s == NS - 1)
    def _():
        for slot in range(5):
            F[slot, H + W :] = jnp.zeros((H, W, 384), BF)

    wide[:, :, :, :, 384:] = jnp.zeros((2, 2, EXT, W, 128), BF)
    for right in (right0, right1):
        right[48:96, 24 * 128 :] = jnp.zeros((W, 128), BF)
        right[96:144, 0:128] = jnp.zeros((W, 128), BF)
    sums[...] = jnp.zeros_like(sums)

    pl.semaphore_wait(barrier, len(greeted))

    def remote(src, dst, send, recv, device):
        return pltpu.make_async_remote_copy(
            src_ref=src, dst_ref=dst, send_sem=send, recv_sem=recv, device_id=device, device_id_type=MESH
        )

    to_east = jnp.where(x < 2, 0, 1)

    def across(side, k, part):
        frame = to_east if side == 0 else 1 - to_east
        low = (0, W - H, H)[part]
        return remote(
            frames.at[frame, low : low + H, :, tiles[k]],
            F.at[3 + side, H + low : H + low + H, :, tiles[k]],
            xs.at[side, k, part],
            xr.at[side, k, part],
            (east if side == 0 else west, s),
        )

    def each_across(ks, parts, act):
        for k in ks:
            for part in parts:
                for side in range(2):
                    act(across(side, k, part))

    def begin(copy):
        copy.start()

    def sent(copy):
        copy.wait_send()

    def received(copy):
        copy.wait_recv()

    outer, inner = (0, 1), (2,)

    def next_across(past, past_parts, ks, parts):
        each_across(past, past_parts, sent)
        each_across(ks, parts, begin)

    sends = (
        ((2,), outer, (1,), outer),
        ((1,), outer, (0,), outer),
        ((0,), outer, (2,), inner),
        ((2,), inner, (1, 0), inner),
    )

    def over():
        return remote(frames.at[1 - core], F.at[2, H : H + W], cs, cr, (twin, s))

    def halo(source, lead, slot, k, way, device_tm):
        low = lead + W - H if way == 0 else lead
        to = 0 if way == 0 else H + W
        return remote(
            source.at[pl.ds(low, H), :, tiles[k]],
            F.at[slot, to : to + H, :, tiles[k]],
            hs.at[slot, way, k],
            hr.at[slot, way, k],
            (device_tm, s + 1 if way == 0 else s - 1),
        )

    has_next = [s < NS - 1, s > 0]
    has_from = [s > 0, s < NS - 1]

    def start_halo(source, lead, slot, k, device_tm, when=None):
        for way in range(2):
            ok = has_next[way] if when is None else has_next[way] & when

            @pl.when(ok)
            def _(way=way):
                halo(source, lead, slot, k, way, device_tm).start()

    def end_halo(source, lead, slot, k, device_tm, when=None):
        for way in range(2):
            ok = has_next[way] if when is None else has_next[way] & when

            @pl.when(ok)
            def _(way=way):
                halo(source, lead, slot, k, way, device_tm).wait_send()

    def got_halo(slot, k, when=None):
        for way in range(2):
            ok = has_from[way] if when is None else has_from[way] & when

            @pl.when(ok)
            def _(way=way):
                halo(F.at[slot], H, slot, k, way, tm).wait_recv()

    own = [frames.at[0], frames.at[1]]

    def meta_copy(side):
        return remote(meta, metas.at[side], ms.at[side], mr.at[side], (east if side == 0 else west, s))

    start_halo(own[1], 0, 1, 2, tm)
    each_across((2,), outer, begin)
    over().start()
    for side in range(2):
        meta_copy(side).start()

    def next_own(k):
        end_halo(own[1], 0, 1, k + 1, tm)
        start_halo(own[1], 0, 1, k, tm)

    def key_copy(o):
        return remote(mine, keys.at[s], ks.at[o - 1], kr.at[o - 1], (tm, lax.rem(s + o, NS)))

    def share_keys():
        for side in range(2):
            meta_copy(side).wait()
        gap = lax.rem(lane((8, 128)), 64) // 16
        third = jnp.where(x == 0, metas[1], jnp.where(x == 1, metas[0], meta[...]))
        mine[...] = jnp.where(gap < 2, meta[...], jnp.where(gap == 2, third, metas[0]))
        to_scalars = pltpu.make_async_copy(mine, scalars, ss)
        to_scalars.start()
        for o in range(1, NS):
            key_copy(o).start()
        keys[s] = mine[...]
        to_scalars.wait()

    def by_x(a, b, c, d):
        return jnp.where(x == 0, a, jnp.where(x == 1, b, jnp.where(x == 2, c, d)))

    firsts = [0, jnp.where(core == 0, 0, 2), by_x(1, 3, 0, 3), by_x(4, 3, 3, 4)]
    seconds = [1, jnp.where(core == 0, 2, 1), by_x(4, 0, 4, 1), by_x(3, 4, 4, 3)]

    def mark_cells():
        for o in range(1, NS):
            key_copy(o).wait()
        for pair in range(NS // 2):
            key = jnp.where(lane((1, 128)) < 64, keys[2 * pair, 3:4], keys[2 * pair + 1, 3:4])
            owner = key // CELLS
            cell = key - owner * CELLS
            there = owner // NS
            row = jnp.where((key >= 0) & (owner - there * NS == s), there * CELLS + cell, -1)

            def put(t, _, pair=pair, row=row):
                number = CELLS * t + lax.broadcasted_iota(jnp.int32, (CELLS, 128), 0)
                hot[pl.ds(pl.multiple_of(CELLS * t, CELLS), CELLS), 128 * pair : 128 * pair + 128] = jnp.where(
                    number == row, 1.0, 0.0
                ).astype(BF)
                return 0

            lax.fori_loop(0, NT, put, 0)

    def stage(pair, k, core_layers=True, rim=True):
        first, second, side = firsts[3], seconds[3], lax.rem(pair, 2)
        for p in range(3):
            first = jnp.where(pair == p, firsts[p], first)
            second = jnp.where(pair == p, seconds[p], second)
        at = pl.ds(pl.multiple_of(128 * k, 128), 128)
        if core_layers:
            for b in range(0, W, 8):
                part = F[first, H + b : H + b + 8, :, at]
                planes[side, 0, b : b + 8, :, at] = part
                planes[side, 1, b : b + 8, :, at] = pltpu.roll(part, 64, 2)
        for b in range(0, EXT, 8):
            if core_layers if H <= b < H + W else rim:
                part = F[second, b : b + 8, :, at]
                wide[side, 0, b : b + 8, :, at] = part
                wide[side, 1, b : b + 8, :, at] = pltpu.roll(part, 64, 2)

    def pass_on(k):
        each_across((k,), outer, received)
        start_halo(own[0], 0, 0, k, tm, x == 1)
        for slot in (3, 4):
            uses = (x == 0) | (x == 3) if slot == 3 else x < 3
            start_halo(F.at[slot], H, slot, k, tm, uses)

    def twin_halos():
        end_halo(own[1], 0, 1, 0, tm)
        for k in (2, 1, 0):
            start_halo(own[0], 0, 2, k, twin, core == 1)

    def own_rim(k):
        if k == 1:
            next_own(0)
        got_halo(1, k)

    def got_twin(k):
        if k == 2:
            over().wait_recv()
        got_halo(2, k, core == 0)

    def got_across(k):
        each_across((k,), inner, received)
        got_halo(0, k, x == 1)
        got_halo(3, k, (x == 0) | (x == 3))
        got_halo(4, k, x < 3)

    def item(i):
        late = i - 30
        pair = jnp.where(i < 15, 0, jnp.where(i < 30, 1, 2 + lax.rem(late + 30, 2)))
        w = jnp.where(i < 15, 14 - i, jnp.where(i < 30, 29 - i, 14 - (late + 30) // 2 + 15))
        return pair, w

    def prepare(i, left, right):
        pair, w = item(i)
        at = 16 * pair + w
        side = lax.rem(pair, 2)
        prepare_first(planes, side, w, right)
        prepare_second(wide, side, w, scalars[0, at], scalars[2, at], left)

    def finish(i, left, right):
        pair, w = item(i)
        at = 16 * pair + w
        correlate(left, right, scalars[1, at], at, sums)

    for i in range(2):
        local(i).wait()
    pltpu.make_async_copy(meta, scalars, ss).wait()

    def own_core(k, _):
        stage(0, k, rim=False)
        return 0

    lax.fori_loop(0, 3, own_core, 0)
    next_own(1)
    got_halo(1, 2)
    stage(0, 2, core_layers=False)
    prepare(0, left0, right0)
    events = [
        (1, functools.partial(own_rim, 1)),
        (2, share_keys),
        (3, twin_halos),
        (4, functools.partial(own_rim, 0)),
        (5, mark_cells),
        (7, functools.partial(got_twin, 2)),
        (8, functools.partial(got_twin, 1)),
        (11, functools.partial(got_twin, 0)),
    ]
    events += [(at, functools.partial(next_across, *send)) for at, send in zip(SEND_STEPS, sends)]
    events += [(at, functools.partial(pass_on, k)) for k, at in PASS_STEPS.items()]
    events += [(at, functools.partial(got_across, k)) for k, at in ((2, 14), (1, 17), (0, 23))]

    def step(h, _):
        for at, event in events:
            pl.when(h == at)(event)

        @pl.when((h == 1) | (h == 4))
        def _():
            stage(0, jnp.where(h == 1, 1, 0), core_layers=False)

        @pl.when((h == 7) | (h == 8) | (h == 11))
        def _():
            stage(1, jnp.where(h == 7, 2, jnp.where(h == 8, 1, 0)))

        @pl.when((h == 14) | (h == 17) | (h == 23))
        def _():
            def both(pair, _):
                stage(pair, jnp.where(h == 14, 2, jnp.where(h == 17, 1, 0)))
                return 0

            lax.fori_loop(2, 4, both, 0)

        prepare(2 * h + 1, left1, right1)
        finish(2 * h, left0, right0)
        prepare(lax.min(2 * h + 2, 59), left0, right0)
        finish(2 * h + 1, left1, right1)
        return 0

    lax.fori_loop(0, 30, step, 0)

    values = velocities(sums, mine[...])
    vector[...] = values

    def vector_copy(o):
        return remote(vector, vectors.at[s], vs.at[o - 1], vr.at[o - 1], (tm, lax.rem(s + o, NS)))

    def vector_beside(side):
        return remote(vector, beside.at[side], bs.at[side], br.at[side], (east if side == 0 else west, s))

    for o in range(1, NS):
        vector_copy(o).start()
    for side in range(2):
        vector_beside(side).start()
    vectors[s] = values
    for o in range(1, NS):
        vector_copy(o).wait_recv()
    rows = jnp.concatenate(
        [
            jnp.where(lane((8, 128)) < 64, vectors[2 * pair], vectors[2 * pair + 1])
            for pair in range(NS // 2)
        ],
        axis=1,
    )
    high = rows.astype(BF).astype(F32)
    middle = (rows - high).astype(BF).astype(F32)
    low = rows - high - middle
    split = jnp.concatenate([high, middle, low, jnp.zeros_like(low)], axis=0).astype(BF)
    cell_sums = lax.dot_general(split, hot[...], (((1,), (1,)), ((), ())), preferred_element_type=F32)
    cell_sums = cell_sums[0:8] + cell_sums[8:16] + cell_sums[16:24]
    for t in range(NT):
        parts[t] = cell_sums[:, CELLS * t : CELLS * t + CELLS]

    def part_copy(o):
        to = lax.rem(tm + o, NT)
        return remote(parts.at[to], arrived.at[tm], ps.at[o - 1], pr.at[o - 1], (to, s))

    for o in range(1, NT):
        part_copy(o).start()
    arrived[tm] = parts[tm]

    for side in range(2):
        vector_beside(side).wait()
    gap = lax.rem(lane((8, 128)), 64) // 16
    third = jnp.where(x == 0, beside[1], jnp.where(x == 1, beside[0], values))
    listed = jnp.where(gap < 2, values, jnp.where(gap == 2, third, beside[1]))
    for a in range(4):
        for i in range(3):
            velocity_out[a, i] = pltpu.roll(listed, 128 - 16 * a, 1)[i : i + 1, :NWIN] if a else listed[i : i + 1, :NWIN]

    for o in range(1, NS):
        vector_copy(o).wait_send()
    over().wait_send()
    each_across((1, 0), inner, sent)
    for k in range(3):
        end_halo(own[0], 0, 2, k, twin, core == 1)
        end_halo(own[0], 0, 0, k, tm, x == 1)
        end_halo(F.at[3], H, 3, k, tm, (x == 0) | (x == 3))
        end_halo(F.at[4], H, 4, k, tm, x < 3)

    for o in range(1, NT):
        part_copy(o).wait()
    total = arrived[0]
    for t in range(1, NT):
        total = total + arrived[t]
    tile_out[...] = total[0:3] / jnp.maximum(total[3:4], 1.0)


def on_device(frames, peak_voxels, owners, tile_cells):
    peaks = jnp.transpose(peak_voxels[:, :, 0, :], (1, 0, 2))
    peaks = jnp.pad(peaks, ((0, 0), (0, 0), (0, 1))).reshape(3, 64)
    key = (owners[:, 0] * CELLS + tile_cells).reshape(4, NWIN)
    key = jnp.pad(key, ((0, 0), (0, 1)), constant_values=-1).reshape(1, 64)
    meta = jnp.pad(jnp.concatenate([peaks, key], axis=0), ((0, 4), (0, 0)))
    meta = jnp.concatenate([meta, meta], axis=1)
    dma = pltpu.SemaphoreType.DMA
    vmem = pltpu.VMEM
    velocity, tile = pl.pallas_call(
        kernel,
        out_shape=[jax.ShapeDtypeStruct((4, 3, 1, NWIN), F32), jax.ShapeDtypeStruct((3, CELLS), F32)],
        in_specs=[pl.BlockSpec(memory_space=pltpu.HBM), pl.BlockSpec(memory_space=vmem)],
        out_specs=[pl.BlockSpec(memory_space=vmem)] * 2,
        scratch_shapes=[
            vmem((5, EXT, W, 384), BF),
            vmem((2, 2, EXT, W, 512), BF),
            vmem((2, 2, W, W, 384), BF),
            vmem((144, DEPTH), BF),
            vmem((144, DEPTH), BF),
            vmem((144, DEPTH), BF),
            vmem((144, DEPTH), BF),
            vmem((6, 64, 128), F32),
            vmem((NT * CELLS, NS * 64), BF),
            vmem((2, 8, 128), jnp.int32),
            vmem((8, 128), jnp.int32),
            pltpu.SMEM((8, 128), jnp.int32),
            vmem((NS, 8, 128), jnp.int32),
            vmem((8, 128), F32),
            vmem((NS, 8, 128), F32),
            vmem((2, 8, 128), F32),
            vmem((NT, 8, 128), F32),
            vmem((NT, 8, 128), F32),
            dma((2,)),
            dma((2, 3, 3)),
            dma((2, 3, 3)),
            dma,
            dma,
            dma((5, 2, 3)),
            dma((5, 2, 3)),
            dma((2,)),
            dma((2,)),
            dma,
            dma((NS - 1,)),
            dma((NS - 1,)),
            dma((NS - 1,)),
            dma((NS - 1,)),
            dma((2,)),
            dma((2,)),
            dma((NT - 1,)),
            dma((NT - 1,)),
        ],
        compiler_params=pltpu.CompilerParams(
            collective_id=0, has_side_effects=True, vmem_limit_bytes=56 * 2**20
        ),
    )(frames, meta)
    return velocity, tile


def solution(mesh):
    placed = (
        P("tm", "space", None, None),
        P(None, None, "tm", "space"),
        P(("tm", "space"), None),
        P(("tm", "space")),
    )
    return jax.shard_map(
        on_device,
        mesh=mesh,
        in_specs=placed,
        out_specs=(P(None, None, "tm", "space"), P(None, ("tm", "space"))),
        check_vma=False,
    )
```

```python
import functools

import jax
import jax.numpy as jnp
from jax import lax
from jax.experimental import pallas as pl
from jax.experimental.pallas import tpu as pltpu
from jax.sharding import PartitionSpec as P

W = 48
STEP = 2
H = 16
S = 24
NWIN = 15
CELLS = 128
NS = 16
NT = 8
EXT = W + 2 * H
BF = jnp.bfloat16
F32 = jnp.float32
MESH = pl.DeviceIdType.MESH

PASS_STEPS = {2: 6, 1: 9, 0: 13}
SEND_STEPS = (2, 7, 12, 14)


def lane(shape):
    return lax.broadcasted_iota(jnp.int32, shape, len(shape) - 1)


def correlate(planes, wide, side, w, qx, qy, qz, row, sums):
    start = S * w
    tile = start // 128
    base = start - 128 * tile
    here = pl.ds(pl.multiple_of(128 * jnp.where(base > 128 - W, tile + 3, tile), 128), 128)
    c = lane((1, 128))
    d = jnp.where(c >= 64, c - 64, c + 64)
    low, high = [lax.rem(v + 128 - base, 128) < W for v in (c, d)]
    zero = jnp.zeros((W, 128), BF)

    def first_pair(x):
        pair = zero if x + 1 == W else jnp.where(high, planes[side, 1, x + 1, :, here], zero)
        return pair if x < 0 else jnp.where(low, planes[side, 0, x, :, here], pair)

    second_tile = (start + 112) // 128
    offset = start + qz - 1 - 128 * (second_tile - 1)
    before = pl.ds(pl.multiple_of(128 * lax.rem(second_tile + 3, 4), 128), 128)
    after = pl.ds(pl.multiple_of(128 * second_tile, 128), 128)
    early, early_turned = c >= offset, d >= offset
    slot = lax.rem(c + 256 - offset, 128) < 64
    turns = [lax.rem(base - offset + 512 - e, 128) for e in range(3)]

    def second_pair(j):
        x = H - 1 + qx + 2 * j
        even = jnp.where(early, wide[side, 0, x, :, before], wide[side, 0, x, :, after])
        odd = jnp.where(early_turned, wide[side, 1, x + 1, :, before], wide[side, 1, x + 1, :, after])
        pair = jnp.where(slot, even, odd)
        return jnp.concatenate([pltpu.roll(pair, turn, 1) for turn in turns], axis=0)

    products, last = None, zero
    for j0 in range(0, 25, STEP):
        left, right = [], []
        for j in range(j0, min(j0 + STEP, 25)):
            left.append(second_pair(j))
            even = first_pair(2 * j) if 2 * j < W else zero
            odd = first_pair(2 * j - 1)
            right.append(jnp.concatenate([odd, even, last], axis=0))
            last = even
        part = lax.dot_general(
            jnp.concatenate(left, axis=1),
            jnp.concatenate(right, axis=1),
            (((1,), (1,)), ((), ())),
            preferred_element_type=F32,
        )
        products = part if products is None else products + part
    c = products
    column = lax.broadcasted_iota(jnp.int32, (W, 144), 1)
    y = jnp.where(column < 48, column, jnp.where(column < 96, column - 48, column - 96))
    lag = lax.broadcasted_iota(jnp.int32, (W, 144), 0) - y - qy

    def diagonal(values, at):
        return jnp.sum(jnp.where(lag == at, values, 0.0), axis=0, keepdims=True)

    def narrow(values, at):
        return jnp.sum(
            jnp.where(lag[:, :128] == at, values[:, :128], 0.0), axis=0, keepdims=True
        )

    centre = diagonal(c[48:96], 0)
    sums[0, pl.ds(row, 1), :] = centre[:, :128]
    sums[1, pl.ds(row, 1), 0:16] = centre[:, 128:144]
    sums[2, pl.ds(row, 1), :] = narrow(c[48:96], -1)
    sums[3, pl.ds(row, 1), :] = narrow(c[48:96], 1)
    sums[4, pl.ds(row, 1), :] = narrow(c[0:48], 0)
    sums[5, pl.ds(row, 1), :] = narrow(c[96:144], 0)


def velocities(sums, peaks):
    c = lane((64, 128))

    def total(k, low, high):
        return jnp.sum(jnp.where((c >= low) & (c < high), sums[k], 0.0), axis=1, keepdims=True)

    columns = (
        total(0, 0, 48),
        total(0, 48, 96),
        total(0, 96, 128) + total(1, 0, 16),
        total(2, 0, 48),
        total(3, 0, 48),
        total(4, 0, 48),
        total(5, 0, 48),
    )
    table = jnp.zeros((64, 128), F32)
    for k, column in enumerate(columns):
        table = jnp.where(c == k, column, table)
    table = jnp.concatenate([table, table], axis=0).T * float(W) ** -1.5
    centre = table[0:1]
    each = lane((1, 128))
    gap = lax.rem(each, 64) // 16
    scale = jnp.where(gap == 0, 1.0, jnp.where(gap == 1, 0.5, jnp.where(gap == 2, 0.25, 0.125)))
    out = jnp.zeros((8, 128), F32)
    row = lax.broadcasted_iota(jnp.int32, (8, 128), 0)
    for axis in range(3):
        lower, upper = table[1 + 2 * axis : 2 + 2 * axis], table[2 + 2 * axis : 3 + 2 * axis]
        curvature = jnp.maximum(2.0 * centre - upper - lower, 1.0)
        value = (peaks[axis : axis + 1].astype(F32) + 0.5 * (upper - lower) / curvature) * scale
        out = jnp.where(row == axis, value, out)
    return jnp.where(row == 3, 1.0, out)


def kernel(
    frames, meta, velocity_out, tile_out,
    F, wide, planes, sums, hot,
    metas, mine, scalars, keys, vector, vectors, beside, parts, arrived,
    local_sem, xs, xr, cs, cr, hs, hr, ms, mr, ss, ks, kr, vs, vr, bs, br, ps, pr,
):
    tm, s = lax.axis_index("tm"), lax.axis_index("space")
    x, core = tm // 2, lax.rem(tm, 2)
    east = 2 * lax.rem(x + 1, 4) + core
    west = 2 * lax.rem(x + 3, 4) + core
    twin = 2 * x + 1 - core
    tiles = [slice(128 * k, 128 * k + 128) for k in range(3)]

    def local(i):
        return pltpu.make_async_copy(frames.at[i], F.at[i, H : H + W], local_sem.at[i])

    for i in range(2):
        local(i).start()
    pltpu.make_async_copy(meta, scalars, ss).start()

    barrier = pltpu.get_barrier_semaphore()
    greeted = [(tm, lax.rem(s + o, NS)) for o in range(1, NS)]
    greeted += [(lax.rem(tm + o, NT), s) for o in range(1, NT)]
    greeted += [(twin, lax.rem(s + 1, NS)), (twin, lax.rem(s + NS - 1, NS))]
    for device in greeted:
        pl.semaphore_signal(barrier, inc=1, device_id=device, device_id_type=MESH)
    @pl.when(s == 0)
    def _():
        for slot in range(5):
            F[slot, 0:H] = jnp.zeros((H, W, 384), BF)

    @pl.when(s == NS - 1)
    def _():
        for slot in range(5):
            F[slot, H + W :] = jnp.zeros((H, W, 384), BF)

    wide[:, :, :, :, 384:] = jnp.zeros((2, 2, EXT, W, 128), BF)
    sums[...] = jnp.zeros_like(sums)

    pl.semaphore_wait(barrier, len(greeted))

    def remote(src, dst, send, recv, device):
        return pltpu.make_async_remote_copy(
            src_ref=src, dst_ref=dst, send_sem=send, recv_sem=recv, device_id=device, device_id_type=MESH
        )

    to_east = jnp.where(x < 2, 0, 1)

    def across(side, k, part):
        frame = to_east if side == 0 else 1 - to_east
        low = (0, W - H, H)[part]
        return remote(
            frames.at[frame, low : low + H, :, tiles[k]],
            F.at[3 + side, H + low : H + low + H, :, tiles[k]],
            xs.at[side, k, part],
            xr.at[side, k, part],
            (east if side == 0 else west, s),
        )

    def each_across(ks, parts, act):
        for k in ks:
            for part in parts:
                for side in range(2):
                    act(across(side, k, part))

    def begin(copy):
        copy.start()

    def sent(copy):
        copy.wait_send()

    def received(copy):
        copy.wait_recv()

    outer, inner = (0, 1), (2,)

    def next_across(past, past_parts, ks, parts):
        each_across(past, past_parts, sent)
        each_across(ks, parts, begin)

    sends = (
        ((2,), outer, (1,), outer),
        ((1,), outer, (0,), outer),
        ((0,), outer, (2,), inner),
        ((2,), inner, (1, 0), inner),
    )

    def over():
        return remote(frames.at[1 - core], F.at[2, H : H + W], cs, cr, (twin, s))

    def halo(source, lead, slot, k, way, device_tm):
        low = lead + W - H if way == 0 else lead
        to = 0 if way == 0 else H + W
        return remote(
            source.at[pl.ds(low, H), :, tiles[k]],
            F.at[slot, to : to + H, :, tiles[k]],
            hs.at[slot, way, k],
            hr.at[slot, way, k],
            (device_tm, s + 1 if way == 0 else s - 1),
        )

    has_next = [s < NS - 1, s > 0]
    has_from = [s > 0, s < NS - 1]

    def start_halo(source, lead, slot, k, device_tm, when=None):
        for way in range(2):
            ok = has_next[way] if when is None else has_next[way] & when

            @pl.when(ok)
            def _(way=way):
                halo(source, lead, slot, k, way, device_tm).start()

    def end_halo(source, lead, slot, k, device_tm, when=None):
        for way in range(2):
            ok = has_next[way] if when is None else has_next[way] & when

            @pl.when(ok)
            def _(way=way):
                halo(source, lead, slot, k, way, device_tm).wait_send()

    def got_halo(slot, k, when=None):
        for way in range(2):
            ok = has_from[way] if when is None else has_from[way] & when

            @pl.when(ok)
            def _(way=way):
                halo(F.at[slot], H, slot, k, way, tm).wait_recv()

    own = [frames.at[0], frames.at[1]]

    def meta_copy(side):
        return remote(meta, metas.at[side], ms.at[side], mr.at[side], (east if side == 0 else west, s))

    start_halo(own[1], 0, 1, 2, tm)
    each_across((2,), outer, begin)
    over().start()
    for side in range(2):
        meta_copy(side).start()

    def next_own(k):
        end_halo(own[1], 0, 1, k + 1, tm)
        start_halo(own[1], 0, 1, k, tm)

    def key_copy(o):
        return remote(mine, keys.at[s], ks.at[o - 1], kr.at[o - 1], (tm, lax.rem(s + o, NS)))

    def share_keys():
        for side in range(2):
            meta_copy(side).wait()
        gap = lax.rem(lane((8, 128)), 64) // 16
        third = jnp.where(x == 0, metas[1], jnp.where(x == 1, metas[0], meta[...]))
        mine[...] = jnp.where(gap < 2, meta[...], jnp.where(gap == 2, third, metas[0]))
        to_scalars = pltpu.make_async_copy(mine, scalars, ss)
        to_scalars.start()
        for o in range(1, NS):
            key_copy(o).start()
        keys[s] = mine[...]
        to_scalars.wait()

    def by_x(a, b, c, d):
        return jnp.where(x == 0, a, jnp.where(x == 1, b, jnp.where(x == 2, c, d)))

    firsts = [0, jnp.where(core == 0, 0, 2), by_x(1, 3, 0, 3), by_x(4, 3, 3, 4)]
    seconds = [1, jnp.where(core == 0, 2, 1), by_x(4, 0, 4, 1), by_x(3, 4, 4, 3)]

    def mark_cells():
        for o in range(1, NS):
            key_copy(o).wait()
        for pair in range(NS // 2):
            key = jnp.where(lane((1, 128)) < 64, keys[2 * pair, 3:4], keys[2 * pair + 1, 3:4])
            owner = key // CELLS
            cell = key - owner * CELLS
            there = owner // NS
            row = jnp.where((key >= 0) & (owner - there * NS == s), there * CELLS + cell, -1)

            def put(t, _, pair=pair, row=row):
                number = CELLS * t + lax.broadcasted_iota(jnp.int32, (CELLS, 128), 0)
                hot[pl.ds(pl.multiple_of(CELLS * t, CELLS), CELLS), 128 * pair : 128 * pair + 128] = jnp.where(
                    number == row, 1.0, 0.0
                ).astype(BF)
                return 0

            lax.fori_loop(0, NT, put, 0)

    def stage(pair, k, core_layers=True, rim=True):
        first, second, side = firsts[3], seconds[3], lax.rem(pair, 2)
        for p in range(3):
            first = jnp.where(pair == p, firsts[p], first)
            second = jnp.where(pair == p, seconds[p], second)
        at, across_at, next_at = [
            pl.ds(pl.multiple_of(128 * t, 128), 128) for t in (k, 3 + lax.min(k, 1), lax.min(k + 1, 2))
        ]
        upper = lane((1, 1, 128)) >= 64
        if core_layers:
            for b in range(0, W, 8):
                part = F[first, H + b : H + b + 8, :, at]
                turned = pltpu.roll(part, 64, 2)
                planes[side, 0, b : b + 8, :, at] = part
                planes[side, 1, b : b + 8, :, at] = turned
                planes[side, 0, b : b + 8, :, across_at] = jnp.where(
                    upper, part, planes[side, 0, b : b + 8, :, next_at]
                )
                planes[side, 1, b : b + 8, :, across_at] = jnp.where(
                    upper, planes[side, 1, b : b + 8, :, next_at], turned
                )
        for b in range(0, EXT, 8):
            if core_layers if H <= b < H + W else rim:
                part = F[second, b : b + 8, :, at]
                wide[side, 0, b : b + 8, :, at] = part
                wide[side, 1, b : b + 8, :, at] = pltpu.roll(part, 64, 2)

    def pass_on(k):
        each_across((k,), outer, received)
        start_halo(own[0], 0, 0, k, tm, x == 1)
        for slot in (3, 4):
            uses = (x == 0) | (x == 3) if slot == 3 else x < 3
            start_halo(F.at[slot], H, slot, k, tm, uses)

    def twin_halos():
        end_halo(own[1], 0, 1, 0, tm)
        for k in (2, 1, 0):
            start_halo(own[0], 0, 2, k, twin, core == 1)

    def own_rim(k):
        if k == 1:
            next_own(0)
        got_halo(1, k)

    def got_twin(k):
        if k == 2:
            over().wait_recv()
        got_halo(2, k, core == 0)

    def got_across(k):
        each_across((k,), inner, received)
        got_halo(0, k, x == 1)
        got_halo(3, k, (x == 0) | (x == 3))
        got_halo(4, k, x < 3)

    def item(i):
        late = i - 30
        pair = jnp.where(i < 15, 0, jnp.where(i < 30, 1, 2 + lax.rem(late + 30, 2)))
        w = jnp.where(i < 15, 14 - i, jnp.where(i < 30, 29 - i, 14 - (late + 30) // 2 + 15))
        return pair, w

    def window(i):
        pair, w = item(i)
        at = 16 * pair + w
        correlate(planes, wide, lax.rem(pair, 2), w, scalars[0, at], scalars[1, at], scalars[2, at], at, sums)

    for i in range(2):
        local(i).wait()
    pltpu.make_async_copy(meta, scalars, ss).wait()

    def own_core(k, _):
        stage(0, 2 - k, rim=False)
        return 0

    lax.fori_loop(0, 3, own_core, 0)
    next_own(1)
    got_halo(1, 2)
    stage(0, 2, core_layers=False)
    events = [
        (1, functools.partial(own_rim, 1)),
        (2, share_keys),
        (3, twin_halos),
        (4, functools.partial(own_rim, 0)),
        (5, mark_cells),
        (7, functools.partial(got_twin, 2)),
        (9, functools.partial(got_twin, 1)),
        (12, functools.partial(got_twin, 0)),
    ]
    events += [(at, functools.partial(next_across, *send)) for at, send in zip(SEND_STEPS, sends)]
    events += [(at, functools.partial(pass_on, k)) for k, at in PASS_STEPS.items()]
    events += [(at, functools.partial(got_across, k)) for k, at in ((2, 15), (1, 18), (0, 24))]

    def step(h, _):
        for at, event in events:
            pl.when(h == at)(event)

        @pl.when((h == 1) | (h == 4))
        def _():
            stage(0, jnp.where(h == 1, 1, 0), core_layers=False)

        @pl.when((h == 7) | (h == 9) | (h == 12))
        def _():
            stage(1, jnp.where(h == 7, 2, jnp.where(h == 9, 1, 0)))

        @pl.when((h == 15) | (h == 18) | (h == 24))
        def _():
            def both(pair, _):
                stage(pair, jnp.where(h == 15, 2, jnp.where(h == 18, 1, 0)))
                return 0

            lax.fori_loop(2, 4, both, 0)

        window(2 * h)
        window(2 * h + 1)
        return 0

    lax.fori_loop(0, 30, step, 0)

    values = velocities(sums, mine[...])
    vector[...] = values

    def vector_copy(o):
        return remote(vector, vectors.at[s], vs.at[o - 1], vr.at[o - 1], (tm, lax.rem(s + o, NS)))

    def vector_beside(side):
        return remote(vector, beside.at[side], bs.at[side], br.at[side], (east if side == 0 else west, s))

    for o in range(1, NS):
        vector_copy(o).start()
    for side in range(2):
        vector_beside(side).start()
    vectors[s] = values
    for o in range(1, NS):
        vector_copy(o).wait_recv()
    rows = jnp.concatenate(
        [
            jnp.where(lane((8, 128)) < 64, vectors[2 * pair], vectors[2 * pair + 1])
            for pair in range(NS // 2)
        ],
        axis=1,
    )
    high = rows.astype(BF).astype(F32)
    middle = (rows - high).astype(BF).astype(F32)
    low = rows - high - middle
    split = jnp.concatenate([high, middle, low, jnp.zeros_like(low)], axis=0).astype(BF)
    cell_sums = lax.dot_general(split, hot[...], (((1,), (1,)), ((), ())), preferred_element_type=F32)
    cell_sums = cell_sums[0:8] + cell_sums[8:16] + cell_sums[16:24]
    for t in range(NT):
        parts[t] = cell_sums[:, CELLS * t : CELLS * t + CELLS]

    def part_copy(o):
        to = lax.rem(tm + o, NT)
        return remote(parts.at[to], arrived.at[tm], ps.at[o - 1], pr.at[o - 1], (to, s))

    for o in range(1, NT):
        part_copy(o).start()
    arrived[tm] = parts[tm]

    for side in range(2):
        vector_beside(side).wait()
    gap = lax.rem(lane((8, 128)), 64) // 16
    third = jnp.where(x == 0, beside[1], jnp.where(x == 1, beside[0], values))
    listed = jnp.where(gap < 2, values, jnp.where(gap == 2, third, beside[1]))
    for a in range(4):
        for i in range(3):
            velocity_out[a, i] = pltpu.roll(listed, 128 - 16 * a, 1)[i : i + 1, :NWIN] if a else listed[i : i + 1, :NWIN]

    for o in range(1, NS):
        vector_copy(o).wait_send()
    over().wait_send()
    each_across((1, 0), inner, sent)
    for k in range(3):
        end_halo(own[0], 0, 2, k, twin, core == 1)
        end_halo(own[0], 0, 0, k, tm, x == 1)
        end_halo(F.at[3], H, 3, k, tm, (x == 0) | (x == 3))
        end_halo(F.at[4], H, 4, k, tm, x < 3)

    for o in range(1, NT):
        part_copy(o).wait()
    total = arrived[0]
    for t in range(1, NT):
        total = total + arrived[t]
    tile_out[...] = total[0:3] / jnp.maximum(total[3:4], 1.0)


def on_device(frames, peak_voxels, owners, tile_cells):
    peaks = jnp.transpose(peak_voxels[:, :, 0, :], (1, 0, 2))
    peaks = jnp.pad(peaks, ((0, 0), (0, 0), (0, 1))).reshape(3, 64)
    key = (owners[:, 0] * CELLS + tile_cells).reshape(4, NWIN)
    key = jnp.pad(key, ((0, 0), (0, 1)), constant_values=-1).reshape(1, 64)
    meta = jnp.pad(jnp.concatenate([peaks, key], axis=0), ((0, 4), (0, 0)))
    meta = jnp.concatenate([meta, meta], axis=1)
    dma = pltpu.SemaphoreType.DMA
    vmem = pltpu.VMEM
    velocity, tile = pl.pallas_call(
        kernel,
        out_shape=[jax.ShapeDtypeStruct((4, 3, 1, NWIN), F32), jax.ShapeDtypeStruct((3, CELLS), F32)],
        in_specs=[pl.BlockSpec(memory_space=pltpu.HBM), pl.BlockSpec(memory_space=vmem)],
        out_specs=[pl.BlockSpec(memory_space=vmem)] * 2,
        scratch_shapes=[
            vmem((5, EXT, W, 384), BF),
            vmem((2, 2, EXT, W, 512), BF),
            vmem((2, 2, W, W, 640), BF),
            vmem((6, 64, 128), F32),
            vmem((NT * CELLS, NS * 64), BF),
            vmem((2, 8, 128), jnp.int32),
            vmem((8, 128), jnp.int32),
            pltpu.SMEM((8, 128), jnp.int32),
            vmem((NS, 8, 128), jnp.int32),
            vmem((8, 128), F32),
            vmem((NS, 8, 128), F32),
            vmem((2, 8, 128), F32),
            vmem((NT, 8, 128), F32),
            vmem((NT, 8, 128), F32),
            dma((2,)),
            dma((2, 3, 3)),
            dma((2, 3, 3)),
            dma,
            dma,
            dma((5, 2, 3)),
            dma((5, 2, 3)),
            dma((2,)),
            dma((2,)),
            dma,
            dma((NS - 1,)),
            dma((NS - 1,)),
            dma((NS - 1,)),
            dma((NS - 1,)),
            dma((2,)),
            dma((2,)),
            dma((NT - 1,)),
            dma((NT - 1,)),
        ],
        compiler_params=pltpu.CompilerParams(
            collective_id=0, has_side_effects=True, vmem_limit_bytes=56 * 2**20
        ),
    )(frames, meta)
    return velocity, tile


def solution(mesh):
    placed = (
        P("tm", "space", None, None),
        P(None, None, "tm", "space"),
        P(("tm", "space"), None),
        P(("tm", "space")),
    )
    return jax.shard_map(
        on_device,
        mesh=mesh,
        in_specs=placed,
        out_specs=(P(None, None, "tm", "space"), P(None, ("tm", "space"))),
        check_vma=False,
    )
```

```python
import functools

import jax
import jax.numpy as jnp
from jax import lax
from jax.experimental import pallas as pl
from jax.experimental.pallas import tpu as pltpu
from jax.sharding import PartitionSpec as P

W = 48
STEP = 2
H = 16
S = 24
NWIN = 15
CELLS = 128
NS = 16
NT = 8
EXT = W + 2 * H
BF = jnp.bfloat16
F32 = jnp.float32
MESH = pl.DeviceIdType.MESH

PASS_STEPS = {2: 6, 1: 9, 0: 14}
SEND_STEPS = (2, 7, 14)


def lane(shape):
    return lax.broadcasted_iota(jnp.int32, shape, len(shape) - 1)


def correlate(planes, wide, side, w, qx, qy, qz, row, sums):
    start = S * w
    tile = start // 128
    base = start - 128 * tile
    here = pl.ds(pl.multiple_of(128 * jnp.where(base > 128 - W, tile + 3, tile), 128), 128)
    c = lane((1, 128))
    d = jnp.where(c >= 64, c - 64, c + 64)
    low, high = [lax.rem(v + 128 - base, 128) < W for v in (c, d)]
    zero = jnp.zeros((W, 128), BF)

    def first_pair(x):
        pair = zero if x + 1 == W else jnp.where(high, planes[side, 1, x + 1, :, here], zero)
        return pair if x < 0 else jnp.where(low, planes[side, 0, x, :, here], pair)

    second_tile = (start + 112) // 128
    offset = start + qz - 1 - 128 * (second_tile - 1)
    before = pl.ds(pl.multiple_of(128 * lax.rem(second_tile + 3, 4), 128), 128)
    after = pl.ds(pl.multiple_of(128 * second_tile, 128), 128)
    early, early_turned = c >= offset, d >= offset
    slot = lax.rem(c + 256 - offset, 128) < 64
    turns = [lax.rem(base - offset + 512 - e, 128) for e in range(3)]

    def second_pair(j):
        x = H - 1 + qx + 2 * j
        even = jnp.where(early, wide[side, 0, x, :, before], wide[side, 0, x, :, after])
        odd = jnp.where(early_turned, wide[side, 1, x + 1, :, before], wide[side, 1, x + 1, :, after])
        pair = jnp.where(slot, even, odd)
        return jnp.concatenate([pltpu.roll(pair, turn, 1) for turn in turns], axis=0)

    products, last = None, zero
    for j0 in range(0, 25, STEP):
        left, right = [], []
        for j in range(j0, min(j0 + STEP, 25)):
            left.append(second_pair(j))
            even = first_pair(2 * j) if 2 * j < W else zero
            odd = first_pair(2 * j - 1)
            right.append(jnp.concatenate([odd, even, last], axis=0))
            last = even
        part = lax.dot_general(
            jnp.concatenate(left, axis=1),
            jnp.concatenate(right, axis=1),
            (((1,), (1,)), ((), ())),
            preferred_element_type=F32,
        )
        products = part if products is None else products + part
    c = products
    column = lax.broadcasted_iota(jnp.int32, (W, 144), 1)
    y = jnp.where(column < 48, column, jnp.where(column < 96, column - 48, column - 96))
    lag = lax.broadcasted_iota(jnp.int32, (W, 144), 0) - y - qy

    def diagonal(values, at):
        return jnp.sum(jnp.where(lag == at, values, 0.0), axis=0, keepdims=True)

    def narrow(values, at):
        return jnp.sum(
            jnp.where(lag[:, :128] == at, values[:, :128], 0.0), axis=0, keepdims=True
        )

    centre = diagonal(c[48:96], 0)
    sums[0, pl.ds(row, 1), :] = centre[:, :128]
    sums[1, pl.ds(row, 1), 0:16] = centre[:, 128:144]
    sums[2, pl.ds(row, 1), :] = narrow(c[48:96], -1)
    sums[3, pl.ds(row, 1), :] = narrow(c[48:96], 1)
    sums[4, pl.ds(row, 1), :] = narrow(c[0:48], 0)
    sums[5, pl.ds(row, 1), :] = narrow(c[96:144], 0)


def velocities(sums, peaks):
    c = lane((64, 128))

    def total(k, low, high):
        return jnp.sum(jnp.where((c >= low) & (c < high), sums[k], 0.0), axis=1, keepdims=True)

    columns = (
        total(0, 0, 48),
        total(0, 48, 96),
        total(0, 96, 128) + total(1, 0, 16),
        total(2, 0, 48),
        total(3, 0, 48),
        total(4, 0, 48),
        total(5, 0, 48),
    )
    table = jnp.zeros((64, 128), F32)
    for k, column in enumerate(columns):
        table = jnp.where(c == k, column, table)
    table = jnp.concatenate([table, table], axis=0).T * float(W) ** -1.5
    centre = table[0:1]
    each = lane((1, 128))
    gap = lax.rem(each, 64) // 16
    scale = jnp.where(gap == 0, 1.0, jnp.where(gap == 1, 0.5, jnp.where(gap == 2, 0.25, 0.125)))
    out = jnp.zeros((8, 128), F32)
    row = lax.broadcasted_iota(jnp.int32, (8, 128), 0)
    for axis in range(3):
        lower, upper = table[1 + 2 * axis : 2 + 2 * axis], table[2 + 2 * axis : 3 + 2 * axis]
        curvature = jnp.maximum(2.0 * centre - upper - lower, 1.0)
        value = (peaks[axis : axis + 1].astype(F32) + 0.5 * (upper - lower) / curvature) * scale
        out = jnp.where(row == axis, value, out)
    return jnp.where(row == 3, 1.0, out)


def kernel(
    frames, meta, velocity_out, tile_out,
    F, wide, planes, sums, hot,
    metas, mine, scalars, keys, vector, vectors, beside, parts, arrived,
    local_sem, xs, xr, cs, cr, hs, hr, ms, mr, ss, ks, kr, vs, vr, bs, br, ps, pr,
):
    tm, s = lax.axis_index("tm"), lax.axis_index("space")
    x, core = tm // 2, lax.rem(tm, 2)
    east = 2 * lax.rem(x + 1, 4) + core
    west = 2 * lax.rem(x + 3, 4) + core
    twin = 2 * x + 1 - core
    tiles = [slice(128 * k, 128 * k + 128) for k in range(3)]

    def local(i):
        return pltpu.make_async_copy(frames.at[i], F.at[i, H : H + W], local_sem.at[i])

    for i in range(2):
        local(i).start()
    pltpu.make_async_copy(meta, scalars, ss).start()

    barrier = pltpu.get_barrier_semaphore()
    greeted = [(tm, lax.rem(s + o, NS)) for o in range(1, NS)]
    greeted += [(lax.rem(tm + o, NT), s) for o in range(1, NT)]
    greeted += [(twin, lax.rem(s + 1, NS)), (twin, lax.rem(s + NS - 1, NS))]
    for device in greeted:
        pl.semaphore_signal(barrier, inc=1, device_id=device, device_id_type=MESH)
    @pl.when(s == 0)
    def _():
        for slot in range(5):
            F[slot, 0:H] = jnp.zeros((H, W, 384), BF)

    @pl.when(s == NS - 1)
    def _():
        for slot in range(5):
            F[slot, H + W :] = jnp.zeros((H, W, 384), BF)

    wide[:, :, :, :, 384:] = jnp.zeros((2, 2, EXT, W, 128), BF)
    sums[...] = jnp.zeros_like(sums)

    pl.semaphore_wait(barrier, len(greeted))

    def remote(src, dst, send, recv, device):
        return pltpu.make_async_remote_copy(
            src_ref=src, dst_ref=dst, send_sem=send, recv_sem=recv, device_id=device, device_id_type=MESH
        )

    to_east = jnp.where(x < 2, 0, 1)

    def across(side, k, part):
        frame = to_east if side == 0 else 1 - to_east
        low = (0, W - H, H)[part]
        return remote(
            frames.at[frame, low : low + H, :, tiles[k]],
            F.at[3 + side, H + low : H + low + H, :, tiles[k]],
            xs.at[side, k, part],
            xr.at[side, k, part],
            (east if side == 0 else west, s),
        )

    def each_across(ks, parts, act):
        for k in ks:
            for part in parts:
                for side in range(2):
                    act(across(side, k, part))

    def begin(copy):
        copy.start()

    def sent(copy):
        copy.wait_send()

    def received(copy):
        copy.wait_recv()

    outer, inner = (0, 1), (2,)

    def next_across(past, following):
        for group in past:
            each_across(*group, sent)
        for group in following:
            each_across(*group, begin)

    sends = (
        ([((2,), outer)], [((1,), outer)]),
        ([((1,), outer)], [((0,), outer), ((2,), inner)]),
        ([((0,), outer), ((2,), inner)], [((1, 0), inner)]),
    )

    def over():
        return remote(frames.at[1 - core], F.at[2, H : H + W], cs, cr, (twin, s))

    def halo(source, lead, slot, k, way, device_tm):
        low = lead + W - H if way == 0 else lead
        to = 0 if way == 0 else H + W
        return remote(
            source.at[pl.ds(low, H), :, tiles[k]],
            F.at[slot, to : to + H, :, tiles[k]],
            hs.at[slot, way, k],
            hr.at[slot, way, k],
            (device_tm, s + 1 if way == 0 else s - 1),
        )

    has_next = [s < NS - 1, s > 0]
    has_from = [s > 0, s < NS - 1]

    def start_halo(source, lead, slot, k, device_tm, when=None):
        for way in range(2):
            ok = has_next[way] if when is None else has_next[way] & when

            @pl.when(ok)
            def _(way=way):
                halo(source, lead, slot, k, way, device_tm).start()

    def end_halo(source, lead, slot, k, device_tm, when=None):
        for way in range(2):
            ok = has_next[way] if when is None else has_next[way] & when

            @pl.when(ok)
            def _(way=way):
                halo(source, lead, slot, k, way, device_tm).wait_send()

    def got_halo(slot, k, when=None):
        for way in range(2):
            ok = has_from[way] if when is None else has_from[way] & when

            @pl.when(ok)
            def _(way=way):
                halo(F.at[slot], H, slot, k, way, tm).wait_recv()

    own = [frames.at[0], frames.at[1]]

    def meta_copy(side):
        return remote(meta, metas.at[side], ms.at[side], mr.at[side], (east if side == 0 else west, s))

    start_halo(own[1], 0, 1, 2, tm)
    each_across((2,), outer, begin)
    over().start()
    for side in range(2):
        meta_copy(side).start()

    def next_own(k):
        end_halo(own[1], 0, 1, k + 1, tm)
        start_halo(own[1], 0, 1, k, tm)

    def key_copy(o):
        return remote(mine, keys.at[s], ks.at[o - 1], kr.at[o - 1], (tm, lax.rem(s + o, NS)))

    def share_keys():
        for side in range(2):
            meta_copy(side).wait()
        gap = lax.rem(lane((8, 128)), 64) // 16
        third = jnp.where(x == 0, metas[1], jnp.where(x == 1, metas[0], meta[...]))
        mine[...] = jnp.where(gap < 2, meta[...], jnp.where(gap == 2, third, metas[0]))
        to_scalars = pltpu.make_async_copy(mine, scalars, ss)
        to_scalars.start()
        for o in range(1, NS):
            key_copy(o).start()
        keys[s] = mine[...]
        to_scalars.wait()

    def by_x(a, b, c, d):
        return jnp.where(x == 0, a, jnp.where(x == 1, b, jnp.where(x == 2, c, d)))

    firsts = [0, jnp.where(core == 0, 0, 2), by_x(1, 3, 0, 3), by_x(4, 3, 3, 4)]
    seconds = [1, jnp.where(core == 0, 2, 1), by_x(4, 0, 4, 1), by_x(3, 4, 4, 3)]

    def mark_cells():
        for o in range(1, NS):
            key_copy(o).wait()
        for pair in range(NS // 2):
            key = jnp.where(lane((1, 128)) < 64, keys[2 * pair, 3:4], keys[2 * pair + 1, 3:4])
            owner = key // CELLS
            cell = key - owner * CELLS
            there = owner // NS
            row = jnp.where((key >= 0) & (owner - there * NS == s), there * CELLS + cell, -1)

            def put(t, _, pair=pair, row=row):
                number = CELLS * t + lax.broadcasted_iota(jnp.int32, (CELLS, 128), 0)
                hot[pl.ds(pl.multiple_of(CELLS * t, CELLS), CELLS), 128 * pair : 128 * pair + 128] = jnp.where(
                    number == row, 1.0, 0.0
                ).astype(BF)
                return 0

            lax.fori_loop(0, NT, put, 0)

    def stage(pair, k, core_layers=True, rim=True):
        first, second, side = firsts[3], seconds[3], lax.rem(pair, 2)
        for p in range(3):
            first = jnp.where(pair == p, firsts[p], first)
            second = jnp.where(pair == p, seconds[p], second)
        at, across_at, next_at = [
            pl.ds(pl.multiple_of(128 * t, 128), 128) for t in (k, 3 + lax.min(k, 1), lax.min(k + 1, 2))
        ]
        upper = lane((1, 1, 128)) >= 64
        if core_layers:
            for b in range(0, W, 8):
                part = F[first, H + b : H + b + 8, :, at]
                turned = pltpu.roll(part, 64, 2)
                planes[side, 0, b : b + 8, :, at] = part
                planes[side, 1, b : b + 8, :, at] = turned
                planes[side, 0, b : b + 8, :, across_at] = jnp.where(
                    upper, part, planes[side, 0, b : b + 8, :, next_at]
                )
                planes[side, 1, b : b + 8, :, across_at] = jnp.where(
                    upper, planes[side, 1, b : b + 8, :, next_at], turned
                )
        for b in range(0, EXT, 8):
            if core_layers if H <= b < H + W else rim:
                part = F[second, b : b + 8, :, at]
                wide[side, 0, b : b + 8, :, at] = part
                wide[side, 1, b : b + 8, :, at] = pltpu.roll(part, 64, 2)

    def pass_on(k):
        each_across((k,), outer, received)
        start_halo(own[0], 0, 0, k, tm, x == 1)
        for slot in (3, 4):
            uses = (x == 0) | (x == 3) if slot == 3 else x < 3
            start_halo(F.at[slot], H, slot, k, tm, uses)

    def twin_halos():
        end_halo(own[1], 0, 1, 0, tm)
        for k in (2, 1, 0):
            start_halo(own[0], 0, 2, k, twin, core == 1)

    def own_rim(k):
        if k == 1:
            next_own(0)
        got_halo(1, k)

    def got_twin(k):
        if k == 2:
            over().wait_recv()
        got_halo(2, k, core == 0)

    def got_across(k):
        each_across((k,), inner, received)
        got_halo(0, k, x == 1)
        got_halo(3, k, (x == 0) | (x == 3))
        got_halo(4, k, x < 3)

    def item(i):
        late = i - 30
        pair = jnp.where(i < 15, 0, jnp.where(i < 30, 1, 2 + lax.rem(late + 30, 2)))
        w = jnp.where(i < 15, 14 - i, jnp.where(i < 30, 29 - i, 14 - (late + 30) // 2 + 15))
        return pair, w

    def window(i):
        pair, w = item(i)
        at = 16 * pair + w
        correlate(planes, wide, lax.rem(pair, 2), w, scalars[0, at], scalars[1, at], scalars[2, at], at, sums)

    for i in range(2):
        local(i).wait()
    pltpu.make_async_copy(meta, scalars, ss).wait()

    def own_core(k, _):
        stage(0, 2 - k, rim=False)
        return 0

    lax.fori_loop(0, 3, own_core, 0)
    next_own(1)
    got_halo(1, 2)
    stage(0, 2, core_layers=False)
    events = [
        (1, functools.partial(own_rim, 1)),
        (2, share_keys),
        (3, twin_halos),
        (4, functools.partial(own_rim, 0)),
        (5, mark_cells),
        (7, functools.partial(got_twin, 2)),
        (9, functools.partial(got_twin, 1)),
        (12, functools.partial(got_twin, 0)),
    ]
    events += [(at, functools.partial(next_across, *send)) for at, send in zip(SEND_STEPS, sends)]
    events += [(at, functools.partial(pass_on, k)) for k, at in PASS_STEPS.items()]
    events += [(at, functools.partial(got_across, k)) for k, at in ((2, 15), (1, 18), (0, 24))]

    def step(h, _):
        for at, event in events:
            pl.when(h == at)(event)

        @pl.when((h == 1) | (h == 4))
        def _():
            stage(0, jnp.where(h == 1, 1, 0), core_layers=False)

        @pl.when((h == 7) | (h == 9) | (h == 12))
        def _():
            stage(1, jnp.where(h == 7, 2, jnp.where(h == 9, 1, 0)))

        @pl.when((h == 15) | (h == 18) | (h == 24))
        def _():
            def both(pair, _):
                stage(pair, jnp.where(h == 15, 2, jnp.where(h == 18, 1, 0)))
                return 0

            lax.fori_loop(2, 4, both, 0)

        window(2 * h)
        window(2 * h + 1)
        return 0

    lax.fori_loop(0, 30, step, 0)

    values = velocities(sums, mine[...])
    vector[...] = values

    def vector_copy(o):
        return remote(vector, vectors.at[s], vs.at[o - 1], vr.at[o - 1], (tm, lax.rem(s + o, NS)))

    def vector_beside(side):
        return remote(vector, beside.at[side], bs.at[side], br.at[side], (east if side == 0 else west, s))

    for o in range(1, NS):
        vector_copy(o).start()
    for side in range(2):
        vector_beside(side).start()
    vectors[s] = values
    for o in range(1, NS):
        vector_copy(o).wait_recv()
    rows = jnp.concatenate(
        [
            jnp.where(lane((8, 128)) < 64, vectors[2 * pair], vectors[2 * pair + 1])
            for pair in range(NS // 2)
        ],
        axis=1,
    )
    high = rows.astype(BF).astype(F32)
    middle = (rows - high).astype(BF).astype(F32)
    low = rows - high - middle
    split = jnp.concatenate([high, middle, low, jnp.zeros_like(low)], axis=0).astype(BF)
    cell_sums = lax.dot_general(split, hot[...], (((1,), (1,)), ((), ())), preferred_element_type=F32)
    cell_sums = cell_sums[0:8] + cell_sums[8:16] + cell_sums[16:24]
    for t in range(NT):
        parts[t] = cell_sums[:, CELLS * t : CELLS * t + CELLS]

    def part_copy(o):
        to = lax.rem(tm + o, NT)
        return remote(parts.at[to], arrived.at[tm], ps.at[o - 1], pr.at[o - 1], (to, s))

    for o in range(1, NT):
        part_copy(o).start()
    arrived[tm] = parts[tm]

    for side in range(2):
        vector_beside(side).wait()
    gap = lax.rem(lane((8, 128)), 64) // 16
    third = jnp.where(x == 0, beside[1], jnp.where(x == 1, beside[0], values))
    listed = jnp.where(gap < 2, values, jnp.where(gap == 2, third, beside[1]))
    for a in range(4):
        for i in range(3):
            velocity_out[a, i] = pltpu.roll(listed, 128 - 16 * a, 1)[i : i + 1, :NWIN] if a else listed[i : i + 1, :NWIN]

    for o in range(1, NS):
        vector_copy(o).wait_send()
    over().wait_send()
    each_across((1, 0), inner, sent)
    for k in range(3):
        end_halo(own[0], 0, 2, k, twin, core == 1)
        end_halo(own[0], 0, 0, k, tm, x == 1)
        end_halo(F.at[3], H, 3, k, tm, (x == 0) | (x == 3))
        end_halo(F.at[4], H, 4, k, tm, x < 3)

    for o in range(1, NT):
        part_copy(o).wait()
    total = arrived[0]
    for t in range(1, NT):
        total = total + arrived[t]
    tile_out[...] = total[0:3] / jnp.maximum(total[3:4], 1.0)


def on_device(frames, peak_voxels, owners, tile_cells):
    peaks = jnp.transpose(peak_voxels[:, :, 0, :], (1, 0, 2))
    peaks = jnp.pad(peaks, ((0, 0), (0, 0), (0, 1))).reshape(3, 64)
    key = (owners[:, 0] * CELLS + tile_cells).reshape(4, NWIN)
    key = jnp.pad(key, ((0, 0), (0, 1)), constant_values=-1).reshape(1, 64)
    meta = jnp.pad(jnp.concatenate([peaks, key], axis=0), ((0, 4), (0, 0)))
    meta = jnp.concatenate([meta, meta], axis=1)
    dma = pltpu.SemaphoreType.DMA
    vmem = pltpu.VMEM
    velocity, tile = pl.pallas_call(
        kernel,
        out_shape=[jax.ShapeDtypeStruct((4, 3, 1, NWIN), F32), jax.ShapeDtypeStruct((3, CELLS), F32)],
        in_specs=[pl.BlockSpec(memory_space=pltpu.HBM), pl.BlockSpec(memory_space=vmem)],
        out_specs=[pl.BlockSpec(memory_space=vmem)] * 2,
        scratch_shapes=[
            vmem((5, EXT, W, 384), BF),
            vmem((2, 2, EXT, W, 512), BF),
            vmem((2, 2, W, W, 640), BF),
            vmem((6, 64, 128), F32),
            vmem((NT * CELLS, NS * 64), BF),
            vmem((2, 8, 128), jnp.int32),
            vmem((8, 128), jnp.int32),
            pltpu.SMEM((8, 128), jnp.int32),
            vmem((NS, 8, 128), jnp.int32),
            vmem((8, 128), F32),
            vmem((NS, 8, 128), F32),
            vmem((2, 8, 128), F32),
            vmem((NT, 8, 128), F32),
            vmem((NT, 8, 128), F32),
            dma((2,)),
            dma((2, 3, 3)),
            dma((2, 3, 3)),
            dma,
            dma,
            dma((5, 2, 3)),
            dma((5, 2, 3)),
            dma((2,)),
            dma((2,)),
            dma,
            dma((NS - 1,)),
            dma((NS - 1,)),
            dma((NS - 1,)),
            dma((NS - 1,)),
            dma((2,)),
            dma((2,)),
            dma((NT - 1,)),
            dma((NT - 1,)),
        ],
        compiler_params=pltpu.CompilerParams(
            collective_id=0, has_side_effects=True, vmem_limit_bytes=56 * 2**20
        ),
    )(frames, meta)
    return velocity, tile


def solution(mesh):
    placed = (
        P("tm", "space", None, None),
        P(None, None, "tm", "space"),
        P(("tm", "space"), None),
        P(("tm", "space")),
    )
    return jax.shard_map(
        on_device,
        mesh=mesh,
        in_specs=placed,
        out_specs=(P(None, None, "tm", "space"), P(None, ("tm", "space"))),
        check_vma=False,
    )
```
